128 devices in a mesh: tm: 16 (over z, y), head: 8 (over x, core).
Axes of the slice: x: 4, y: 4, z: 4, core: 2. Of those that a mesh axis runs over, the one named last changes fastest.
Arguments:
- query: bfloat16 [4096, 3072], P(('tm', 'head')), may hold values from -100 to 100
- key_cur: bfloat16 [4096, 3072], P(('tm', 'head')), may hold values from -6 to 6
- value_cur: bfloat16 [4096, 3072], P(('tm', 'head')), may hold values from -6 to 6
- d_out: bfloat16 [4096, 3072], P(('tm', 'head')), may hold values from -6 to 6
- key_hist: bfloat16 [4096, 3072], P('tm', 'head'), may hold values from -10 to 10
- value_hist: bfloat16 [4096, 3072], P('tm', 'head'), may hold values from -6 to 6
- hist_len: int32 [16], P('tm'), may hold values from 1 to 256, 2048 in all
Outputs:
- grad_query: bfloat16 [4096, 3072], P(('tm', 'head'))
- grad_key_cur: bfloat16 [4096, 3072], P(('tm', 'head'))
- grad_value_cur: bfloat16 [4096, 3072], P(('tm', 'head'))
- grad_key_hist: bfloat16 [4096, 3072], P('tm', 'head')
- grad_value_hist: bfloat16 [4096, 3072], P('tm', 'head')
The draws below stay inside these ranges and needn't reach their ends.
Inputs may be any that keep to these rules, and one draw needn't show every extreme that they name: `hist_len`: every time shard has at least one filled slot; filled slots come first.
All inputs are finite; a program needn't handle non-finite values.
Results may differ from the reference program's by a relative error of at most 0.019.
Values may be sent and summed in bfloat16 or wider, within the bound.
No kernel may reach another device: no remote copies, remote signals or barrier semaphores. Data moves between devices by JAX's collectives and lax.ppermute only.
A program may use at most 128 MiB of HBM per device.

```python
import math
import jax
import jax.numpy as jnp
import numpy as np
from jax import lax

D = 3072
HEADS = 24
HS = 128
HIST_DEV = 256
TOKENS = 4096
HIST = 4096
N_TM = 16


def shared_keys(key):
    base_keys = jax.random.normal(key, (HIST, D), jnp.float32)
    return jnp.clip(base_keys, -6.0, 6.0)


def draw_key_hist(key, part):
    key_table = shared_keys(key)
    return jnp.clip(key_table, -10.0, 10.0).astype(jnp.bfloat16)


def draw_query(key, part):
    key = jax.random.fold_in(key, 3)
    drawn = jnp.clip(jax.random.normal(key, (TOKENS, D), jnp.float32), -6.0, 6.0)
    return drawn.astype(jnp.bfloat16)


def level_of(rng, dims, pieces, low, top_value):
    gain, own = 1.0, jax.random.fold_in(rng, 6)
    for dim, shards_of in pieces:
        draws = jnp.exp(jax.random.uniform(jax.random.fold_in(own, dim), (shards_of,), jnp.float32, low / len(pieces), top_value / len(pieces)))
        gain = gain * jnp.repeat(draws, dims[dim] // shards_of).reshape([-1 if axis == dim else 1 for axis in range(len(dims))])
    return gain


def split_up(count, total, most, lean):
    weights = [(1 << 20) // math.isqrt(rank ** lean) + 1 for rank in range(2, count + 1)]
    rest, holding = total - most - (count - 1), [1] * (count - 1)
    while rest > 0:
        free = [i for i in range(count - 1) if holding[i] < most]
        pool, left = sum([weights[i] for i in free]), rest
        for i in free:
            more = min(most - holding[i], max(1, left * weights[i] // pool), rest)
            holding[i] = holding[i] + more
            rest = rest - more
    return np.array([most] + holding)


def uneven_parts(stream_key, count, total, most, skew):
    if count == 2:
        one = jax.random.randint(stream_key, (), max(1, total - most), min(most, total - 1) + 1)
        return jnp.stack([one, total - one])
    lengths = jnp.asarray(split_up(count, total, most, skew), jnp.int32)
    couples = (count - 1) // 2
    source_of, sink = lengths[1:1 + 2 * couples:2], lengths[2:2 + 2 * couples:2]
    slack = jnp.minimum(source_of - 1, most - sink)
    passed = jax.random.randint(jax.random.fold_in(stream_key, 1), (couples,), 0, 1 << 20) % (slack + 1)
    lengths = lengths.at[1:1 + 2 * couples:2].set(source_of - passed).at[2:2 + 2 * couples:2].set(sink + passed)
    return lengths[jax.random.permutation(jax.random.fold_in(stream_key, 2), count)]


def scatter_about(key, dims, deviation, limit, cuts=(), held_as=jnp.bfloat16):
    loudness = level_of(key, dims, cuts, -0.22, 0.18) if cuts else 1.0
    values = jax.random.normal(key, dims, jnp.float32) * deviation * loudness
    return jnp.minimum(jnp.maximum(values, -limit), limit).astype(held_as)


def setup_inputs(seed: int = 0) -> dict:
    key_list = jax.random.split(jax.random.key(seed), 8)
    query = draw_query(jax.random.fold_in(key_list[7], 71), 0)
    key_cur = scatter_about(key_list[1], (TOKENS, D), 1.0, 6.0, ((0, 128),))
    value_cur = scatter_about(key_list[2], (TOKENS, D), 1.0, 6.0, ((0, 128),))
    d_out = scatter_about(key_list[3], (TOKENS, D), 1.0, 6.0, ((0, 128),))
    key_hist = draw_key_hist(jax.random.fold_in(key_list[7], 71), 0)
    value_hist = scatter_about(key_list[5], (HIST, D), 1.0, 6.0, ((0, 16), (1, 8)))
    hist_len = uneven_parts(key_list[6], N_TM, HIST_DEV * N_TM // 2, HIST_DEV, 2).astype(jnp.int32)
    return dict(query=query, key_cur=key_cur, value_cur=value_cur, d_out=d_out, key_hist=key_hist, value_hist=value_hist, hist_len=hist_len)


def reference(query, key_cur, value_cur, d_out, key_hist, value_hist, hist_len):
    score_scale = 1.0 / math.sqrt(HS)
    slot_index = jnp.arange(HIST)
    live_hist = slot_index % HIST_DEV < hist_len[slot_index // HIST_DEV]
    live_mask = jnp.concatenate([jnp.ones((TOKENS,), dtype=bool), live_hist])
    all_keys = jnp.concatenate([key_cur, key_hist], axis=0)
    all_values = jnp.concatenate([value_cur, value_hist], axis=0)

    def by_heads(array):
        return array.reshape(array.shape[0], HEADS, HS).transpose(1, 0, 2)

    def head_grads(inputs):
        query_head, key_head, value_head, grad_head = inputs
        scores = jnp.dot(query_head, key_head.T, preferred_element_type=jnp.float32) * score_scale
        row_max = lax.optimization_barrier(jnp.max(jnp.where(live_mask[None, :], scores, -jnp.inf), axis=1, keepdims=True))
        weights = jnp.where(live_mask[None, :], jnp.exp(scores - row_max), 0.0)
        row_total = lax.optimization_barrier(jnp.sum(weights, axis=1, keepdims=True))
        grad_scores = jnp.dot(grad_head, value_head.T, preferred_element_type=jnp.float32)
        row_delta = lax.optimization_barrier(jnp.sum(weights * grad_scores, axis=1, keepdims=True)) / row_total
        full_prob = weights / row_total
        prob_low = full_prob.astype(jnp.bfloat16)
        score_grad = (score_scale * full_prob * (grad_scores - row_delta)).astype(jnp.bfloat16)
        grad_q = jnp.dot(score_grad, key_head, preferred_element_type=jnp.float32).astype(jnp.bfloat16)
        grad_k = jnp.dot(score_grad.T, query_head, preferred_element_type=jnp.float32).astype(jnp.bfloat16)
        grad_v = jnp.dot(prob_low.T, grad_head, preferred_element_type=jnp.float32).astype(jnp.bfloat16)
        return (grad_q, grad_k, grad_v)
    grad_q, grad_k, grad_v = lax.map(head_grads, (by_heads(query), by_heads(all_keys), by_heads(all_values), by_heads(d_out)))

    def joined(array):
        return array.transpose(1, 0, 2).reshape(array.shape[1], D)
    grad_q = joined(grad_q)
    grad_k = joined(grad_k)
    grad_v = joined(grad_v)
    return (grad_q, grad_k[:TOKENS], grad_v[:TOKENS], grad_k[TOKENS:], grad_v[TOKENS:])
```

```python
import math

import jax
import jax.numpy as jnp
from jax import lax
from jax.experimental import pallas as pl
from jax.experimental.pallas import tpu as pltpu
from jax.sharding import Mesh
from jax.sharding import PartitionSpec as P

HS = 128
SCALE = 1.0 / math.sqrt(HS)
EXP2_SCALE = SCALE * math.log2(math.e)
LOW = -1e30
VMEM_LIMIT = 48 * 1024 * 1024
AXES = ("z", "y", "x", "c")
F32 = jnp.float32
BF16 = jnp.bfloat16


def rows_dot(a, b):
    return lax.dot_general(a, b, (((1,), (1,)), ((), ())), preferred_element_type=F32)


def plain_dot(a, b):
    return lax.dot_general(a, b, (((1,), (0,)), ((), ())), preferred_element_type=F32)


def left_dot(a, b):
    return lax.dot_general(a, b, (((0,), (0,)), ((), ())), preferred_element_type=F32)


def load_all(sources, targets, sem):
    copies = [
        pltpu.make_async_copy(s, t, sem.at[i]) for i, (s, t) in enumerate(zip(sources, targets))
    ]
    for copy in copies:
        copy.start()
    for copy in copies:
        copy.wait()


def live_mask(hist_buf, block, rows, width):
    count = hist_buf[block, 2 * rows : 2 * rows + 16, 0:width].astype(F32)[0:1]
    slot = lax.broadcasted_iota(jnp.int32, (rows, width), 0).astype(F32)
    return slot < count


def stat_step(keys, values, queries, grads, state, mask):
    top, total, dots = state
    scores = rows_dot(keys, queries)
    if mask is not None:
        scores = jnp.where(mask, scores, LOW)
    new_top = jnp.maximum(top, jnp.max(scores, axis=0, keepdims=True))
    shrink = jnp.exp2((top - new_top) * EXP2_SCALE)
    weights = jnp.exp2((scores - new_top) * EXP2_SCALE)
    grad_scores = rows_dot(values, grads)
    total = total * shrink + jnp.sum(weights, axis=0, keepdims=True)
    dots = dots * shrink + jnp.sum(weights * grad_scores, axis=0, keepdims=True)
    return new_top, total, dots


def stat_kernel(nk, nq, todo, *refs):
    cur_in, hist_in, query_in = refs[:nk], refs[nk : 2 * nk], refs[2 * nk : 2 * nk + nq]
    rest = refs[2 * nk + nq :]
    has_state = any(not fresh for fresh, _ in todo)
    if has_state:
        state_in, rest = rest[0], rest[1:]
    out_ref, cur, hist, query, sem = rest
    load_all(
        list(cur_in) + list(hist_in) + list(query_in),
        [cur.at[i] for i in range(nk)]
        + [hist.at[i] for i in range(nk)]
        + [query.at[i] for i in range(nq)],
        sem,
    )
    rows = cur.shape[2]
    width = query.shape[2]
    heads = cur.shape[3] // HS

    def one(head, block, fresh, key_blocks):
        lanes = pl.ds(pl.multiple_of(head * HS, HS), HS)
        queries, grads = query[block, 0, :, lanes], query[block, 1, :, lanes]
        row = head * 4 + block
        if fresh:
            state = (
                jnp.full((1, width), LOW, F32),
                jnp.zeros((1, width), F32),
                jnp.zeros((1, width), F32),
            )
        else:
            state = tuple(state_in[i, pl.ds(row, 1), :] for i in range(3))
        for kb in key_blocks:
            state = stat_step(
                cur[kb, 0, :, lanes], cur[kb, 1, :, lanes], queries, grads, state, None
            )
            state = stat_step(
                hist[kb, 0:rows, lanes],
                hist[kb, rows : 2 * rows, lanes],
                queries,
                grads,
                state,
                live_mask(hist, kb, rows, width),
            )
        for i in range(3):
            out_ref[i, pl.ds(row, 1), :] = state[i]

    groups = []
    for block, (fresh, key_blocks) in enumerate(todo):
        if groups and groups[-1][1:] == (fresh, key_blocks):
            groups[-1][0].append(block)
        else:
            groups.append(([block], fresh, key_blocks))
    for blocks, fresh, key_blocks in groups:
        first, count = blocks[0], len(blocks)

        def step(i, _, first=first, count=count, fresh=fresh, key_blocks=key_blocks):
            one(i // count, first + i % count, fresh, key_blocks)
            return 0

        lax.fori_loop(0, heads * count, step, 0)


def stats_call(curs, hists, queries, todo, state=None):
    nk, nq = len(curs), len(queries)
    rows, width = curs[0].shape[1], queries[0].shape[1]
    feat = curs[0].shape[2]
    any_spec = pl.BlockSpec(memory_space=pl.ANY)
    vmem = pl.BlockSpec(memory_space=pltpu.VMEM)
    args = list(curs) + list(hists) + list(queries)
    in_specs = [any_spec] * len(args)
    if state is not None:
        args.append(state)
        in_specs.append(vmem)
    pairs = sum(len(k) for _, k in todo)
    flops = 2 * 2 * pairs * (2 * rows) * width * feat

    def kernel(*refs):
        stat_kernel(nk, nq, todo, *refs)

    return pl.pallas_call(
        kernel,
        out_shape=jax.ShapeDtypeStruct((3, 16, width), F32),
        in_specs=in_specs,
        out_specs=vmem,
        scratch_shapes=[
            pltpu.VMEM((nk, 2, rows, feat), BF16),
            pltpu.VMEM((nk, 2 * rows + 16, feat), BF16),
            pltpu.VMEM((nq, 2, width, feat), BF16),
            pltpu.SemaphoreType.DMA((2 * nk + nq,)),
        ],
        compiler_params=pltpu.CompilerParams(vmem_limit_bytes=VMEM_LIMIT),
        cost_estimate=pl.CostEstimate(
            flops=2 * flops,
            bytes_accessed=sum(a.size * a.dtype.itemsize for a in args),
            transcendentals=pairs * 2 * rows * width * (feat // HS),
        ),
    )(*args)


OFFSETS = (0, -1, 1, 2)


def combine_stats(stats, base_ref, delta_ref, heads):
    for head in range(heads):
        for block, offset in enumerate(OFFSETS):
            parts = []
            for ref, step in zip(stats, OFFSETS):
                there = [o % 4 for o in OFFSETS].index((offset - step) % 4)
                row = head * 4 + there
                parts.append([ref[i, row : row + 1, :] for i in range(3)])
            top = jnp.maximum(
                jnp.maximum(parts[0][0], parts[1][0]), jnp.maximum(parts[2][0], parts[3][0])
            )
            total = jnp.zeros_like(top)
            dots = jnp.zeros_like(top)
            for part in parts:
                shrink = jnp.exp2((part[0] - top) * EXP2_SCALE)
                total = total + part[1] * shrink
                dots = dots + part[2] * shrink
            row = head * 4 + block
            base_ref[row : row + 1, :] = top + jnp.log2(total) * (1.0 / EXP2_SCALE)
            delta_ref[row : row + 1, :] = dots / total


def grad_kernel(nk, nq, last, *refs):
    cur_in, hist_in, query_in = refs[:nk], refs[nk : 2 * nk], refs[2 * nk : 2 * nk + nq]
    refs = refs[2 * nk + nq :]
    stats, refs = refs[:4], refs[4:]
    sum_in = None
    if len(refs) > 2 * nk + 1 + 9:
        sum_in, refs = refs[0], refs[1:]
    cur_out, hist_out, sum_out = refs[:nk], refs[nk : 2 * nk], refs[2 * nk]
    cur, hist, query, cur_grad, hist_grad, sums, base, delta, sem = refs[2 * nk + 1 :]
    load_all(
        list(cur_in) + list(hist_in) + list(query_in),
        [cur.at[i] for i in range(nk)]
        + [hist.at[i] for i in range(nk)]
        + [query.at[i] for i in range(nq)],
        sem,
    )
    rows = cur.shape[2]
    width = query.shape[2]
    heads = cur.shape[3] // HS
    combine_stats(stats, base, delta, heads)
    if sum_in is None:
        sums[...] = jnp.zeros_like(sums)
    else:
        sums[...] = sum_in[...]

    def part(head, lanes, keys, values, mask):
        grad_k = grad_v = None
        for block in range(nq):
            queries, grads = query[block, 0, :, lanes], query[block, 1, :, lanes]
            row = pl.ds(head * 4 + block, 1)
            scores = rows_dot(keys, queries)
            prob = jnp.exp2((scores - base[row, :]) * EXP2_SCALE)
            if mask is not None:
                prob = jnp.where(mask, prob, 0.0)
            grad_scores = rows_dot(values, grads)
            score_grad = (prob * (grad_scores - delta[row, :])).astype(BF16)
            add_v = plain_dot(prob.astype(BF16), grads)
            add_k = plain_dot(score_grad, queries)
            grad_v = add_v if grad_v is None else grad_v + add_v
            grad_k = add_k if grad_k is None else grad_k + add_k
            sums[block, :, lanes] += left_dot(score_grad, keys)
        return (grad_k * SCALE).astype(BF16), grad_v.astype(BF16)

    def step(i, _):
        head, kb = i // nk, i % nk
        lanes = pl.ds(pl.multiple_of(head * HS, HS), HS)
        grad_k, grad_v = part(head, lanes, cur[kb, 0, :, lanes], cur[kb, 1, :, lanes], None)
        cur_grad[kb, 0, :, lanes] = grad_k
        cur_grad[kb, 1, :, lanes] = grad_v
        grad_k, grad_v = part(
            head,
            lanes,
            hist[kb, 0:rows, lanes],
            hist[kb, rows : 2 * rows, lanes],
            live_mask(hist, kb, rows, width),
        )
        hist_grad[kb, 0, :, lanes] = grad_k
        hist_grad[kb, 1, :, lanes] = grad_v
        return 0

    lax.fori_loop(0, heads * nk, step, 0)
    if last:
        sum_out[...] = (sums[...] * SCALE).astype(BF16)
    else:
        sum_out[...] = sums[...]
    load_all(
        [cur_grad.at[i] for i in range(nk)] + [hist_grad.at[i] for i in range(nk)],
        list(cur_out) + list(hist_out),
        sem,
    )


def grads_call(curs, hists, queries, stats, sums=None, last=False):
    nk, nq = len(curs), len(queries)
    rows, width = curs[0].shape[1], queries[0].shape[1]
    feat = curs[0].shape[2]
    any_spec = pl.BlockSpec(memory_space=pl.ANY)
    vmem = pl.BlockSpec(memory_space=pltpu.VMEM)
    args = list(curs) + list(hists) + list(queries)
    in_specs = [any_spec] * len(args)
    args += list(stats)
    in_specs += [vmem] * 4
    if sums is not None:
        args.append(sums)
        in_specs.append(vmem)
    block = jax.ShapeDtypeStruct((2, rows, feat), BF16)
    flops = 5 * 2 * nk * nq * (2 * rows) * width * feat

    def kernel(*refs):
        grad_kernel(nk, nq, last, *refs)

    outs = pl.pallas_call(
        kernel,
        out_shape=[block] * (2 * nk)
        + [jax.ShapeDtypeStruct((nq, width, feat), BF16 if last else F32)],
        in_specs=in_specs,
        out_specs=[any_spec] * (2 * nk) + [vmem],
        scratch_shapes=[
            pltpu.VMEM((nk, 2, rows, feat), BF16),
            pltpu.VMEM((nk, 2 * rows + 16, feat), BF16),
            pltpu.VMEM((nq, 2, width, feat), BF16),
            pltpu.VMEM((nk, 2, rows, feat), BF16),
            pltpu.VMEM((nk, 2, rows, feat), BF16),
            pltpu.VMEM((nq, width, feat), F32),
            pltpu.VMEM((16, width), F32),
            pltpu.VMEM((16, width), F32),
            pltpu.SemaphoreType.DMA((2 * nk + nq,)),
        ],
        compiler_params=pltpu.CompilerParams(vmem_limit_bytes=VMEM_LIMIT),
        cost_estimate=pl.CostEstimate(
            flops=2 * flops,
            bytes_accessed=sum(a.size * a.dtype.itemsize for a in args),
            transcendentals=nk * nq * 2 * rows * width * (feat // HS),
        ),
    )(*args)
    return outs[:nk], outs[nk : 2 * nk], outs[2 * nk]


def ring_moves(sizes):
    nz, ny, nx, nc = sizes

    def table(target):
        pairs = []
        for z in range(nz):
            for y in range(ny):
                for x in range(nx):
                    for c in range(nc):
                        tz, ty = target(z, y, c)
                        src = ((z * ny + y) * nx + x) * nc + c
                        pairs.append((src, (((tz % nz) * ny + ty % ny) * nx + x) * nc + c))
        return pairs

    def keys(step):
        return table(lambda z, y, c: (z, y + step) if c == 0 else (z + step, y))

    def queries(step):
        return table(lambda z, y, c: (z + step, y) if c == 0 else (z, y + step))

    return keys, queries


def make_shards(sizes):
    key_move, query_move = ring_moves(sizes)

    def to_key(value, step):
        return lax.ppermute(value, AXES, key_move(step))

    def to_query(value, step):
        return lax.ppermute(value, AXES, query_move(step))

    def shards(query, key_cur, value_cur, d_out, key_hist, value_hist, hist_len):
        tokens = query.shape[0]
        head_dev = sizes[2] * sizes[3]
        feat = key_hist.shape[1]
        rows = key_hist.shape[0]
        count = jnp.broadcast_to(hist_len.astype(BF16)[:, None], (16, feat))
        hist0 = jnp.concatenate([key_hist, value_hist, count], axis=0)
        hist_m, hist_p = to_key(hist0, 1), to_key(hist0, -1)
        hist2 = to_key(hist_m, 1)

        packed = jnp.stack([query, d_out, key_cur, value_cur])
        packed = packed.reshape(4, tokens, head_dev, feat).transpose(2, 0, 1, 3)
        moved = lax.all_to_all(
            packed.reshape(head_dev, 4 * tokens, feat), ("x", "c"), 0, 0, tiled=True
        )
        moved = moved.reshape(head_dev, 4, tokens, feat).transpose(1, 0, 2, 3)
        moved = moved.reshape(4, head_dev * tokens, feat)
        query0, cur0 = moved[:2], moved[2:]

        cur_m, cur_p = to_key(cur0, 1), to_key(cur0, -1)
        query_m, query_p = to_query(query0, 1), to_query(query0, -1)
        cur2 = to_key(cur_p, -1)
        query2 = jnp.stack([to_query(query_p[0], -1), to_query(query_m[1], 1)])

        curs, hists = [cur0, cur_m, cur_p, cur2], [hist0, hist_m, hist_p, hist2]
        queries = [query0, query_m, query_p, query2]
        state = stats_call(curs[:3], hists[:3], queries[:3], [(True, (0, 1, 2))] * 3)
        state = stats_call(
            curs, hists, queries, [(False, (3,))] * 3 + [(True, (0, 1, 2, 3))], state
        )
        stats = [state, to_query(state, 1), to_query(state, -1), to_query(state, 2)]

        far_cur, far_hist, sums = grads_call(curs[3:], hists[3:], queries, stats)
        got_cur, got_hist = to_key(far_cur[0], 1), to_key(far_hist[0], -1)
        near_cur, near_hist, sums = grads_call(curs[1:3], hists[1:3], queries, stats, sums)
        send_cur_p = (near_cur[1].astype(F32) + got_cur.astype(F32)).astype(BF16)
        send_hist_m = (near_hist[0].astype(F32) + got_hist.astype(F32)).astype(BF16)
        cur_a, cur_b = to_key(send_cur_p, 1), to_key(near_cur[0], -1)
        hist_a, hist_b = to_key(near_hist[1], 1), to_key(send_hist_m, -1)
        own_cur, own_hist, sums = grads_call(
            curs[:1], hists[:1], queries, stats, sums, last=True
        )
        query_a, query_b, query_c = (
            to_query(sums[1], -1),
            to_query(sums[2], 1),
            to_query(sums[3], 2),
        )

        def total(*parts):
            return sum(part.astype(F32) for part in parts).astype(BF16)

        grad_query = total(sums[0], query_a, query_b, query_c)
        grad_cur = total(own_cur[0], cur_a, cur_b)
        grad_hist = total(own_hist[0], hist_a, hist_b)
        back = jnp.concatenate([grad_query[None], grad_cur], axis=0)
        back = back.reshape(3, head_dev, tokens, feat).transpose(1, 0, 2, 3)
        back = lax.all_to_all(
            back.reshape(head_dev, 3 * tokens, feat), ("x", "c"), 0, 0, tiled=True
        )
        back = back.reshape(head_dev, 3, tokens, feat).transpose(1, 2, 0, 3)
        back = back.reshape(3, tokens, head_dev * feat)
        return back[0], back[1], back[2], grad_hist[0], grad_hist[1]

    return shards


def solution(mesh):
    sizes = (4, 4, 4, 2)
    grid = Mesh(mesh.devices.reshape(sizes), AXES)
    token = P(AXES, None)
    hist = P(("z", "y"), ("x", "c"))
    return jax.shard_map(
        make_shards(sizes),
        mesh=grid,
        in_specs=(token, token, token, token, hist, hist, P(("z", "y"))),
        out_specs=(token, token, token, hist, hist),
        check_vma=False,
    )
```

```python
import math

import jax
import jax.numpy as jnp
from jax import lax
from jax.experimental import pallas as pl
from jax.experimental.pallas import tpu as pltpu
from jax.sharding import Mesh
from jax.sharding import PartitionSpec as P

HS = 128
SCALE = 1.0 / math.sqrt(HS)
EXP2_SCALE = SCALE * math.log2(math.e)
LOW = -1e30
VMEM_LIMIT = 24 * 1024 * 1024
AXES = ("z", "y", "x", "c")
OFFSETS = (0, -1, 1, 2)
F32 = jnp.float32
BF16 = jnp.bfloat16
VMEM = pl.BlockSpec(memory_space=pltpu.VMEM)


def rows_dot(a, b):
    return lax.dot_general(a, b, (((1,), (1,)), ((), ())), preferred_element_type=F32)


def plain_dot(a, b):
    return lax.dot_general(a, b, (((1,), (0,)), ((), ())), preferred_element_type=F32)


def call(kernel, outs, args, flops=0, exps=0, scratch=()):
    size = sum(a.size * a.dtype.itemsize for a in args)
    return pl.pallas_call(
        kernel,
        out_shape=outs,
        in_specs=[VMEM] * len(args),
        out_specs=jax.tree.map(lambda _: VMEM, outs),
        scratch_shapes=list(scratch),
        compiler_params=pltpu.CompilerParams(vmem_limit_bytes=VMEM_LIMIT),
        cost_estimate=pl.CostEstimate(flops=flops // 64, bytes_accessed=size // 64, transcendentals=0),
    )(*args)


def head_lanes(head):
    return pl.ds(pl.multiple_of(head * HS, HS), HS)


def dead_bias(hist, rows, width):
    count = hist[2 * rows : 2 * rows + 16, 0:HS].astype(F32)[0:1]
    slot = lax.broadcasted_iota(jnp.int32, (rows, HS), 0).astype(F32)
    bias = jnp.where(slot < count, 0.0, LOW)
    return jnp.concatenate([bias] * (width // HS), axis=1)


def wide(refs, which, lanes):
    return jnp.concatenate([ref[which, :, lanes] for ref in refs], axis=0)


def stat_step(keys, values, queries, grads, state, bias):
    top, total, dots = state
    scores = rows_dot(keys, queries)
    if bias is not None:
        scores = scores + bias
    new_top = jnp.maximum(top, jnp.max(scores, axis=0, keepdims=True))
    shrink = jnp.exp2((top - new_top) * EXP2_SCALE)
    weights = jnp.exp2((scores - new_top) * EXP2_SCALE)
    grad_scores = rows_dot(values, grads)
    total = total * shrink + jnp.sum(weights, axis=0, keepdims=True)
    dots = dots * shrink + jnp.sum(weights * grad_scores, axis=0, keepdims=True)
    return new_top, total, dots


def stats_call(curs, hists, queries, groups, state_in=None):
    nk, nq = len(curs), len(queries)
    rows, feat = curs[0].shape[1:]
    tokens = queries[0].shape[1]
    heads = feat // HS

    def kernel(*refs):
        cur, hist, query = refs[:nk], refs[nk : 2 * nk], refs[2 * nk : 2 * nk + nq]
        old, out = refs[2 * nk + nq], refs[-1]

        def step(head, _):
            lanes = head_lanes(head)
            for blocks, key_blocks, fresh in groups:
                width = tokens * len(blocks)
                queries = wide([query[b] for b in blocks], 0, lanes)
                grads = wide([query[b] for b in blocks], 1, lanes)
                if fresh:
                    state = (
                        jnp.full((1, width), LOW, F32),
                        jnp.zeros((1, width), F32),
                        jnp.zeros((1, width), F32),
                    )
                else:
                    state = tuple(
                        jnp.concatenate(
                            [old[i, pl.ds(head * 4 + b, 1), :] for b in blocks], axis=1
                        )
                        for i in range(3)
                    )
                for kb in key_blocks:
                    state = stat_step(
                        cur[kb][0, :, lanes], cur[kb][1, :, lanes], queries, grads, state, None
                    )
                    state = stat_step(
                        hist[kb][0:rows, lanes],
                        hist[kb][rows : 2 * rows, lanes],
                        queries,
                        grads,
                        state,
                        dead_bias(hist[kb], rows, width),
                    )
                for i in range(3):
                    for j, b in enumerate(blocks):
                        out[i, pl.ds(head * 4 + b, 1), :] = state[i][
                            :, j * tokens : (j + 1) * tokens
                        ]
            return 0

        lax.fori_loop(0, heads, step, 0)

    args = list(curs) + list(hists) + list(queries) + ([] if state_in is None else [state_in])
    pairs = sum(len(b) * len(k) for b, k, _ in groups)
    work = pairs * 2 * rows * tokens
    out = jax.ShapeDtypeStruct((3, 16, tokens), F32)
    return call(kernel, out, args, flops=2 * 2 * 2 * work * feat, exps=work * heads)


def combine_stats(stats, base_ref, delta_ref, heads):
    for head in range(heads):
        for block, offset in enumerate(OFFSETS):
            parts = []
            for ref, step in zip(stats, OFFSETS):
                there = [o % 4 for o in OFFSETS].index((offset - step) % 4)
                row = head * 4 + there
                parts.append([ref[i, row : row + 1, :] for i in range(3)])
            top = jnp.maximum(
                jnp.maximum(parts[0][0], parts[1][0]), jnp.maximum(parts[2][0], parts[3][0])
            )
            total = jnp.zeros_like(top)
            dots = jnp.zeros_like(top)
            for part in parts:
                shrink = jnp.exp2((part[0] - top) * EXP2_SCALE)
                total = total + part[1] * shrink
                dots = dots + part[2] * shrink
            at = slice(block * top.shape[1], (block + 1) * top.shape[1])
            base_ref[head, 0:1, at] = top + jnp.log2(total) * (1.0 / EXP2_SCALE)
            delta_ref[head, 0:1, at] = dots / total


def grads_call(curs, hists, queries, stats, sums_in=None, far=None):
    nk, nq = len(curs), len(queries)
    rows, feat = curs[0].shape[1:]
    tokens = queries[0].shape[1]
    heads = feat // HS
    width = nq * tokens
    last = far is not None

    def kernel(*refs):
        cur, hist, query = refs[:nk], refs[nk : 2 * nk], refs[2 * nk : 2 * nk + nq]
        refs = refs[2 * nk + nq :]
        stat, refs = refs[:4], refs[4:]
        if sums_in is not None:
            old, refs = refs[0], refs[1:]
        if last:
            far_in, refs = refs[0], refs[1:]
        key_out, sum_out = refs[:nk], refs[nk:-2]
        base, delta = refs[-2:]
        combine_stats(stat, base, delta, heads)

        def part(keys, values, queries, grads, lift, shift, bias):
            scores = rows_dot(keys, queries) - lift
            if bias is not None:
                scores = scores + bias
            prob = jnp.exp2(scores * EXP2_SCALE)
            grad_scores = rows_dot(values, grads)
            score_grad = (prob * (grad_scores - shift)).astype(BF16)
            grad_v = plain_dot(prob.astype(BF16), grads)
            grad_k = plain_dot(score_grad, queries) * SCALE
            return score_grad, grad_k, grad_v

        def store(kb, i, lanes, value):
            if last:
                value = value + far_in[i, :, lanes].astype(F32)
            key_out[kb][i, :, lanes] = value.astype(BF16)

        def step(head, _):
            lanes = head_lanes(head)
            queries, grads = wide(query, 0, lanes), wide(query, 1, lanes)
            lift, shift = base[head, 0:1, :], delta[head, 0:1, :]
            total = None if sums_in is None else old[head]
            for kb in range(nk):
                keys = cur[kb][0, :, lanes]
                score_a, grad_k, grad_v = part(
                    keys, cur[kb][1, :, lanes], queries, grads, lift, shift, None
                )
                store(kb, 0, lanes, grad_k)
                store(kb, 1, lanes, grad_v)
                old_keys = hist[kb][0:rows, lanes]
                score_b, grad_k, grad_v = part(
                    old_keys,
                    hist[kb][rows : 2 * rows, lanes],
                    queries,
                    grads,
                    lift,
                    shift,
                    dead_bias(hist[kb], rows, width),
                )
                store(kb, 2, lanes, grad_k)
                store(kb, 3, lanes, grad_v)
                add = plain_dot(
                    jnp.concatenate([keys, old_keys], axis=0).T,
                    jnp.concatenate([score_a, score_b], axis=0),
                )
                total = add if total is None else total + add
            if last:
                for b in range(nq):
                    piece = total[:, b * tokens : (b + 1) * tokens] * SCALE
                    sum_out[b][:, lanes] = piece.T.astype(BF16)
            else:
                sum_out[0][head] = total
            return 0

        lax.fori_loop(0, heads, step, 0)

    block = jax.ShapeDtypeStruct((4, rows, feat), BF16)
    if last:
        sums = [jax.ShapeDtypeStruct((tokens, feat), BF16)] * nq
    else:
        sums = [jax.ShapeDtypeStruct((heads, HS, width), F32)]
    args = list(curs) + list(hists) + list(queries) + list(stats)
    args += [a for a in (sums_in, far) if a is not None]
    work = nk * 2 * rows * width
    outs = call(
        kernel,
        [block] * nk + sums,
        args,
        flops=2 * 5 * 2 * work * feat,
        exps=work * heads,
        scratch=[pltpu.VMEM((heads, 8, width), F32)] * 2,
    )
    return list(outs[:nk]), list(outs[nk:])


def pack_call(arrays, parts):
    rows, columns = arrays[0].shape
    feat = columns // parts

    def kernel(*refs):
        out = refs[-1]
        for i, ref in enumerate(refs[:-1]):
            for p in range(parts):
                out[p, i * rows : (i + 1) * rows, :] = ref[:, p * feat : (p + 1) * feat]

    shape = jax.ShapeDtypeStruct((parts, len(arrays) * rows, feat), BF16)
    return call(kernel, shape, arrays)


def unpack_call(array, count):
    parts, rows, feat = array.shape
    rows //= count

    def kernel(ref, *outs):
        for i, out in enumerate(outs):
            for p in range(parts):
                out[:, p * feat : (p + 1) * feat] = ref[p, i * rows : (i + 1) * rows, :]

    return call(kernel, [jax.ShapeDtypeStruct((rows, parts * feat), BF16)] * count, [array])


def split_call(array, count):
    parts, rows, feat = array.shape
    rows //= count

    def kernel(ref, *outs):
        for i in range(count):
            for p in range(parts):
                outs[i // 2][i % 2, p * rows : (p + 1) * rows, :] = ref[
                    p, i * rows : (i + 1) * rows, :
                ]

    block = jax.ShapeDtypeStruct((2, parts * rows, feat), BF16)
    return call(kernel, [block] * (count // 2), [array])


def add_call(query_parts, cur_parts, parts):
    tokens, feat = query_parts[0].shape
    rows = tokens // parts
    nq = len(query_parts)

    def kernel(*refs):
        out = refs[-1]
        sums = [
            sum(ref[...].astype(F32) for ref in refs[:nq]),
            sum(ref[0].astype(F32) for ref in refs[nq:-1]),
            sum(ref[1].astype(F32) for ref in refs[nq:-1]),
        ]
        for i, total in enumerate(sums):
            low = total.astype(BF16)
            for p in range(parts):
                out[p, i * rows : (i + 1) * rows, :] = low[p * rows : (p + 1) * rows]

    shape = jax.ShapeDtypeStruct((parts, 3 * rows, feat), BF16)
    return call(kernel, shape, list(query_parts) + list(cur_parts))


def add_hist_call(key_parts):
    _, rows, feat = key_parts[0].shape

    def kernel(*refs):
        for i, out in enumerate(refs[-2:]):
            out[...] = sum(ref[2 + i].astype(F32) for ref in refs[:-2]).astype(BF16)

    return call(kernel, [jax.ShapeDtypeStruct((rows, feat), BF16)] * 2, list(key_parts))


def ring_moves(sizes):
    nz, ny, nx, nc = sizes

    def table(target):
        pairs = []
        for z in range(nz):
            for y in range(ny):
                for x in range(nx):
                    for c in range(nc):
                        tz, ty = target(z, y, c)
                        src = ((z * ny + y) * nx + x) * nc + c
                        pairs.append((src, (((tz % nz) * ny + ty % ny) * nx + x) * nc + c))
        return pairs

    def keys(step):
        return table(lambda z, y, c: (z, y + step) if c == 0 else (z + step, y))

    def queries(step):
        return table(lambda z, y, c: (z + step, y) if c == 0 else (z, y + step))

    return keys, queries


def make_shards(sizes):
    key_move, query_move = ring_moves(sizes)

    def to_key(value, step):
        return lax.ppermute(value, AXES, key_move(step))

    def to_query(value, step):
        return lax.ppermute(value, AXES, query_move(step))

    def shards(query, key_cur, value_cur, d_out, key_hist, value_hist, hist_len):
        parts = sizes[2] * sizes[3]
        feat = key_hist.shape[1]
        count = jnp.broadcast_to(hist_len.astype(BF16)[:, None], (16, feat))
        hist0 = jnp.concatenate([key_hist, value_hist, count], axis=0)
        hists = [hist0] + [to_key(hist0, -o) for o in OFFSETS[1:]]

        packed = pack_call([query, d_out, key_cur, value_cur], parts)
        moved = lax.all_to_all(packed, ("x", "c"), 0, 0, tiled=True)
        moved, hists = lax.optimization_barrier((moved, hists))
        query0, cur0 = split_call(moved, 4)

        curs = [cur0] + [to_key(cur0, -o) for o in OFFSETS[1:]]
        queries = [query0] + [to_query(query0, -o) for o in OFFSETS[1:]]
        near = (0, 1, 2)
        state = stats_call(curs[:3], hists[:3], queries[:3], [(near, near, True)])
        state = stats_call(
            curs, hists, queries, [(near, (3,), False), ((3,), (0, 1, 2, 3), True)], state
        )
        stats = [state] + [to_query(state, -o) for o in OFFSETS[1:]]

        far, sums = grads_call(curs[3:], hists[3:], queries, stats)
        far = to_key(far[0], 2)
        near, sums = grads_call(curs[1:3], hists[1:3], queries, stats, sums[0])
        near = [to_key(block, offset) for block, offset in zip(near, OFFSETS[1:3])]
        own, sums = grads_call(curs[:1], hists[:1], queries, stats, sums[0], far)
        query_parts = [sums[0]] + [to_query(sums[i], OFFSETS[i]) for i in range(1, 4)]

        back = add_call(query_parts, own + near, parts)
        back = lax.all_to_all(back, ("x", "c"), 0, 0, tiled=True)
        outs = unpack_call(back, 3)
        grad_k, grad_v = add_hist_call(own + near)
        return outs[0], outs[1], outs[2], grad_k, grad_v

    return shards


def solution(mesh):
    sizes = (4, 4, 4, 2)
    grid = Mesh(mesh.devices.reshape(sizes), AXES)
    token = P(AXES, None)
    hist = P(("z", "y"), ("x", "c"))
    return jax.shard_map(
        make_shards(sizes),
        mesh=grid,
        in_specs=(token, token, token, token, hist, hist, P(("z", "y"))),
        out_specs=(token, token, token, hist, hist),
        check_vma=False,
    )
```

```python
import math

import jax
import jax.numpy as jnp
from jax import lax
from jax.experimental import pallas as pl
from jax.experimental.pallas import tpu as pltpu
from jax.sharding import Mesh
from jax.sharding import PartitionSpec as P

HS = 128
SCALE = 1.0 / math.sqrt(HS)
EXP2_SCALE = SCALE * math.log2(math.e)
LOW = -1e30
VMEM_LIMIT = 24 * 1024 * 1024
PACK_LIMIT = 56 * 1024 * 1024
AXES = ("z", "y", "x", "c")
OFFSETS = (0, -1, 1, 2)
F32 = jnp.float32
BF16 = jnp.bfloat16
VMEM = pl.BlockSpec(memory_space=pltpu.VMEM)


def rows_dot(a, b):
    return lax.dot_general(a, b, (((1,), (1,)), ((), ())), preferred_element_type=F32)


def plain_dot(a, b):
    return lax.dot_general(a, b, (((1,), (0,)), ((), ())), preferred_element_type=F32)


def call(kernel, outs, args, flops=0, exps=0, scratch=()):
    size = sum(a.size * a.dtype.itemsize for a in args)
    return pl.pallas_call(
        kernel,
        out_shape=outs,
        in_specs=[VMEM] * len(args),
        out_specs=jax.tree.map(lambda _: VMEM, outs),
        scratch_shapes=list(scratch),
        compiler_params=pltpu.CompilerParams(vmem_limit_bytes=VMEM_LIMIT),
        cost_estimate=pl.CostEstimate(flops=flops // 64, bytes_accessed=size // 64, transcendentals=0),
    )(*args)


def head_lanes(head):
    return pl.ds(pl.multiple_of(head * HS, HS), HS)


def dead_bias(hist, rows, width):
    count = hist[2 * rows : 2 * rows + 16, 0:HS].astype(F32)[0:1]
    slot = lax.broadcasted_iota(jnp.int32, (rows, HS), 0).astype(F32)
    bias = jnp.where(slot < count, 0.0, LOW)
    return jnp.concatenate([bias] * (width // HS), axis=1)


def flatten(blocks):
    return [a for block in blocks for a in (block if isinstance(block, list) else [block])]


def regroup(refs, blocks):
    refs = list(refs)
    return [[refs.pop(0) for _ in block] if isinstance(block, list) else refs.pop(0) for block in blocks]


def take(block, which, lanes):
    return block[which][:, lanes] if isinstance(block, list) else block[which, :, lanes]


def wide(blocks, which, lanes):
    return jnp.concatenate([take(block, which, lanes) for block in blocks], axis=0)


def stat_step(keys, values, queries, grads, state, bias):
    top, total, dots = state
    scores = rows_dot(keys, queries)
    if bias is not None:
        scores = scores + bias
    new_top = jnp.maximum(top, jnp.max(scores, axis=0, keepdims=True))
    shrink = jnp.exp2((top - new_top) * EXP2_SCALE)
    weights = jnp.exp2((scores - new_top) * EXP2_SCALE)
    grad_scores = rows_dot(values, grads)
    total = total * shrink + jnp.sum(weights, axis=0, keepdims=True)
    dots = dots * shrink + jnp.sum(weights * grad_scores, axis=0, keepdims=True)
    return new_top, total, dots


def stats_call(curs, hists, queries, groups, state_in=None):
    nk, nh, nq = len(flatten(curs)), len(hists), len(flatten(queries))
    rows, feat = hists[0].shape[0] // 2 - 8, hists[0].shape[1]
    tokens = queries[0].shape[1]
    heads = feat // HS

    def kernel(*refs):
        cur, hist = regroup(refs[:nk], curs), refs[nk : nk + nh]
        query = regroup(refs[nk + nh : nk + nh + nq], queries)
        old, out = refs[nk + nh + nq], refs[-1]

        def step(head, _):
            lanes = head_lanes(head)
            for blocks, cur_blocks, hist_blocks, fresh in groups:
                width = tokens * len(blocks)
                asked = wide([query[b] for b in blocks], 0, lanes)
                grads = wide([query[b] for b in blocks], 1, lanes)
                if fresh:
                    state = (
                        jnp.full((1, width), LOW, F32),
                        jnp.zeros((1, width), F32),
                        jnp.zeros((1, width), F32),
                    )
                else:
                    state = tuple(
                        jnp.concatenate(
                            [old[i, pl.ds(head * 4 + b, 1), :] for b in blocks], axis=1
                        )
                        for i in range(3)
                    )
                for kb in cur_blocks:
                    state = stat_step(
                        take(cur[kb], 0, lanes), take(cur[kb], 1, lanes), asked, grads, state, None
                    )
                for kb in hist_blocks:
                    state = stat_step(
                        hist[kb][0:rows, lanes],
                        hist[kb][rows : 2 * rows, lanes],
                        asked,
                        grads,
                        state,
                        dead_bias(hist[kb], rows, width),
                    )
                for i in range(3):
                    for j, b in enumerate(blocks):
                        out[i, pl.ds(head * 4 + b, 1), :] = state[i][
                            :, j * tokens : (j + 1) * tokens
                        ]
            return 0

        lax.fori_loop(0, heads, step, 0)

    args = flatten(curs) + list(hists) + flatten(queries) + ([] if state_in is None else [state_in])
    work = sum(len(b) * (len(c) + len(h)) for b, c, h, _ in groups) * rows * tokens
    out = jax.ShapeDtypeStruct((3, 16, tokens), F32)
    return call(kernel, out, args, flops=2 * 2 * 2 * work * feat, exps=work * heads)


def combine_stats(stats, base_ref, delta_ref, heads):
    for head in range(heads):
        for block, offset in enumerate(OFFSETS):
            parts = []
            for ref, step in zip(stats, OFFSETS):
                there = [o % 4 for o in OFFSETS].index((offset - step) % 4)
                row = head * 4 + there
                parts.append([ref[i, row : row + 1, :] for i in range(3)])
            top = jnp.maximum(
                jnp.maximum(parts[0][0], parts[1][0]), jnp.maximum(parts[2][0], parts[3][0])
            )
            total = jnp.zeros_like(top)
            dots = jnp.zeros_like(top)
            for part in parts:
                shrink = jnp.exp2((part[0] - top) * EXP2_SCALE)
                total = total + part[1] * shrink
                dots = dots + part[2] * shrink
            at = slice(block * top.shape[1], (block + 1) * top.shape[1])
            base_ref[head, 0:1, at] = top + jnp.log2(total) * (1.0 / EXP2_SCALE)
            delta_ref[head, 0:1, at] = dots / total


def grads_call(curs, hists, queries, stats, sums_in=None, far=None):
    nk, nq = len(curs), len(queries)
    rows, feat = hists[0].shape[0] // 2 - 8, hists[0].shape[1]
    tokens = queries[0].shape[1]
    heads = feat // HS
    width = nq * tokens
    n_cur, n_query = len(flatten(curs)), len(flatten(queries))
    last = far is not None

    def kernel(*refs):
        cur, refs = regroup(refs[:n_cur], curs), refs[n_cur:]
        hist, refs = refs[:nk], refs[nk:]
        query, refs = regroup(refs[:n_query], queries), refs[n_query:]
        stat, refs = refs[:4], refs[4:]
        if sums_in is not None:
            old, refs = refs[0], refs[1:]
        if last:
            far_in, refs = refs[0], refs[1:]
        key_out, sum_out = refs[:nk], refs[nk:-2]
        base, delta = refs[-2:]
        combine_stats(stat, base, delta, heads)

        def part(keys, values, queries, grads, lift, shift, bias):
            scores = rows_dot(keys, queries) - lift
            if bias is not None:
                scores = scores + bias
            prob = jnp.exp2(scores * EXP2_SCALE)
            grad_scores = rows_dot(values, grads)
            score_grad = (prob * (grad_scores - shift)).astype(BF16)
            grad_v = plain_dot(prob.astype(BF16), grads)
            grad_k = plain_dot(score_grad, queries) * SCALE
            return score_grad, grad_k, grad_v

        def store(kb, i, lanes, value):
            if last:
                value = value + far_in[i, :, lanes].astype(F32)
            key_out[kb][i, :, lanes] = value.astype(BF16)

        def step(head, _):
            lanes = head_lanes(head)
            asked, grads = wide(query, 0, lanes), wide(query, 1, lanes)
            lift, shift = base[head, 0:1, :], delta[head, 0:1, :]
            total = None if sums_in is None else old[head]
            for kb in range(nk):
                keys = take(cur[kb], 0, lanes)
                score_a, grad_k, grad_v = part(
                    keys, take(cur[kb], 1, lanes), asked, grads, lift, shift, None
                )
                store(kb, 0, lanes, grad_k)
                store(kb, 1, lanes, grad_v)
                old_keys = hist[kb][0:rows, lanes]
                score_b, grad_k, grad_v = part(
                    old_keys,
                    hist[kb][rows : 2 * rows, lanes],
                    asked,
                    grads,
                    lift,
                    shift,
                    dead_bias(hist[kb], rows, width),
                )
                store(kb, 2, lanes, grad_k)
                store(kb, 3, lanes, grad_v)
                add = plain_dot(
                    jnp.concatenate([keys, old_keys], axis=0).T,
                    jnp.concatenate([score_a, score_b], axis=0),
                )
                total = add if total is None else total + add
            if last:
                for b in range(nq):
                    piece = total[:, b * tokens : (b + 1) * tokens] * SCALE
                    sum_out[b][:, lanes] = piece.T.astype(BF16)
            else:
                sum_out[0][head] = total
            return 0

        lax.fori_loop(0, heads, step, 0)

    block = jax.ShapeDtypeStruct((4, rows, feat), BF16)
    if last:
        sums = [jax.ShapeDtypeStruct((tokens, feat), BF16)] * nq
    else:
        sums = [jax.ShapeDtypeStruct((heads, HS, width), F32)]
    args = flatten(curs) + list(hists) + flatten(queries) + list(stats)
    args += [a for a in (sums_in, far) if a is not None]
    work = nk * 2 * rows * width
    outs = call(
        kernel,
        [block] * nk + sums,
        args,
        flops=2 * 5 * 2 * work * feat,
        exps=work * heads,
        scratch=[pltpu.VMEM((heads, 8, width), F32)] * 2,
    )
    return list(outs[:nk]), list(outs[nk:])


def pack_call(arrays, key_hist, value_hist, hist_len, parts):
    rows, columns = arrays[0].shape
    feat = columns // parts
    old = key_hist.shape[0]
    n = len(arrays)

    def kernel(*refs):
        ins, (key_in, value_in, count), outs = refs[:n], refs[n : n + 3], refs[n + 3 :]
        outs, (hist, held, sem) = outs[:-3], outs[-3:]
        copies = [pltpu.make_async_copy(ref, held.at[i], sem.at[i]) for i, ref in enumerate(ins)]
        copies.append(pltpu.make_async_copy(key_in, hist.at[pl.ds(0, old)], sem.at[n]))
        copies.append(pltpu.make_async_copy(value_in, hist.at[pl.ds(old, old)], sem.at[n + 1]))
        for copy in copies:
            copy.start()
        filled = jnp.full((16, feat), count[0], jnp.int32).astype(F32)
        hist[2 * old :, :] = filled.astype(BF16)
        for i in range(n):
            copies[i].wait()
            for p in range(parts):
                outs[i // 2][p, i % 2 * rows : (i % 2 + 1) * rows, :] = held[
                    i, :, p * feat : (p + 1) * feat
                ]
        copies[n].wait()
        copies[n + 1].wait()

    pair = jax.ShapeDtypeStruct((parts, 2 * rows, feat), BF16)
    return pl.pallas_call(
        kernel,
        out_shape=[pair] * (n // 2) + [jax.ShapeDtypeStruct((2 * old + 16, feat), BF16)],
        in_specs=[pl.BlockSpec(memory_space=pl.ANY)] * (n + 2)
        + [pl.BlockSpec(memory_space=pltpu.SMEM)],
        out_specs=[VMEM] * (n // 2 + 1),
        scratch_shapes=[
            pltpu.VMEM((n, rows, columns), BF16),
            pltpu.SemaphoreType.DMA((n + 2,)),
        ],
        compiler_params=pltpu.CompilerParams(vmem_limit_bytes=PACK_LIMIT),
    )(*arrays, key_hist, value_hist, hist_len)


def split_call(array, count):
    parts, rows, feat = array.shape
    rows //= count

    def kernel(ref, *outs):
        for i in range(count):
            for p in range(parts):
                outs[i // 2][i % 2, p * rows : (p + 1) * rows, :] = ref[
                    p, i * rows : (i + 1) * rows, :
                ]

    block = jax.ShapeDtypeStruct((2, parts * rows, feat), BF16)
    return call(kernel, [block] * (count // 2), [array])


def unpack_call(array, count):
    parts, rows, feat = array.shape
    rows //= count

    def kernel(ref, *outs):
        for i, out in enumerate(outs):
            for p in range(parts):
                out[:, p * feat : (p + 1) * feat] = ref[p, i * rows : (i + 1) * rows, :]

    return call(kernel, [jax.ShapeDtypeStruct((rows, parts * feat), BF16)] * count, [array])


def add_call(query_parts, cur_parts, parts):
    tokens, feat = query_parts[0].shape
    rows = tokens // parts
    nq = len(query_parts)

    def kernel(*refs):
        out = refs[-1]
        sums = [
            sum(ref[...].astype(F32) for ref in refs[:nq]),
            sum(ref[0].astype(F32) for ref in refs[nq:-1]),
            sum(ref[1].astype(F32) for ref in refs[nq:-1]),
        ]
        for i, total in enumerate(sums):
            low = total.astype(BF16)
            for p in range(parts):
                out[p, i * rows : (i + 1) * rows, :] = low[p * rows : (p + 1) * rows]

    shape = jax.ShapeDtypeStruct((parts, 3 * rows, feat), BF16)
    return call(kernel, shape, list(query_parts) + list(cur_parts))


def add_hist_call(key_parts):
    _, rows, feat = key_parts[0].shape

    def kernel(*refs):
        for i, out in enumerate(refs[-2:]):
            out[...] = sum(ref[2 + i].astype(F32) for ref in refs[:-2]).astype(BF16)

    return call(kernel, [jax.ShapeDtypeStruct((rows, feat), BF16)] * 2, list(key_parts))


def ring_moves(sizes):
    nz, ny, nx, nc = sizes

    def table(target):
        pairs = []
        for z in range(nz):
            for y in range(ny):
                for x in range(nx):
                    for c in range(nc):
                        tz, ty, tx, tc = target(z, y, x, c)
                        src = ((z * ny + y) * nx + x) * nc + c
                        dst = ((tz % nz) * ny + ty % ny) * nx + tx % nx
                        pairs.append((src, dst * nc + tc % nc))
        return pairs

    def keys(step):
        return table(lambda z, y, x, c: (z, y + step, x, c) if c == 0 else (z + step, y, x, c))

    def queries(step):
        return table(lambda z, y, x, c: (z + step, y, x, c) if c == 0 else (z, y + step, x, c))

    return keys, queries


def make_shards(sizes):
    key_move, query_move = ring_moves(sizes)

    def to_key(value, step):
        return lax.ppermute(value, AXES, key_move(step))

    def to_query(value, step):
        return lax.ppermute(value, AXES, query_move(step))

    def shards(query, key_cur, value_cur, d_out, key_hist, value_hist, hist_len):
        parts = sizes[2] * sizes[3]
        asked, kept, hist0 = pack_call(
            [query, d_out, key_cur, value_cur], key_hist, value_hist, hist_len, parts
        )
        hists = [hist0] + [to_key(hist0, -o) for o in OFFSETS[1:]]
        asked = lax.all_to_all(asked, ("x", "c"), 0, 0, tiled=True)
        kept, asked = lax.optimization_barrier((kept, asked))
        kept = lax.all_to_all(kept, ("x", "c"), 0, 0, tiled=True)
        query0 = split_call(asked, 2)[0]
        queries = [query0] + [to_query(query0, -o) for o in OFFSETS[1:]]
        cur0 = split_call(kept, 2)[0]
        curs = [cur0] + [to_key(cur0, -o) for o in OFFSETS[1:]]
        every = (0, 1, 2, 3)
        state = stats_call(curs[:1], hists, queries, [(every, (0,), every, True)])
        state = stats_call(curs, hists[:1], queries, [(every, (1, 2, 3), (), False)], state)
        stats = [state] + [to_query(state, -o) for o in OFFSETS[1:]]

        far, sums = grads_call(curs[3:], hists[3:], queries, stats)
        far = to_key(far[0], 2)
        near, sums = grads_call(curs[1:3], hists[1:3], queries, stats, sums[0])
        near = [to_key(block, offset) for block, offset in zip(near, OFFSETS[1:3])]
        own, sums = grads_call(curs[:1], hists[:1], queries, stats, sums[0], far)
        query_parts = [sums[0]] + [to_query(sums[i], OFFSETS[i]) for i in range(1, 4)]

        back = add_call(query_parts, own + near, parts)
        back = lax.all_to_all(back, ("x", "c"), 0, 0, tiled=True)
        outs = unpack_call(back, 3)
        grad_k, grad_v = add_hist_call(own + near)
        return outs[0], outs[1], outs[2], grad_k, grad_v

    return shards


def solution(mesh):
    sizes = (4, 4, 4, 2)
    grid = Mesh(mesh.devices.reshape(sizes), AXES)
    token = P(AXES, None)
    hist = P(("z", "y"), ("x", "c"))
    return jax.shard_map(
        make_shards(sizes),
        mesh=grid,
        in_specs=(token, token, token, token, hist, hist, P(("z", "y"))),
        out_specs=(token, token, token, hist, hist),
        check_vma=False,
    )
```

```python
import math

import jax
import jax.numpy as jnp
from jax import lax
from jax.experimental import pallas as pl
from jax.experimental.pallas import tpu as pltpu
from jax.sharding import Mesh
from jax.sharding import PartitionSpec as P

HS = 128
SCALE = 1.0 / math.sqrt(HS)
EXP2_SCALE = SCALE * math.log2(math.e)
LOW = -1e30
VMEM_LIMIT = 24 * 1024 * 1024
PACK_LIMIT = 56 * 1024 * 1024
AXES = ("z", "y", "x", "c")
OFFSETS = (0, -1, 1, 2)
X_STEPS = (0, 1, 3, 2)
F32 = jnp.float32
BF16 = jnp.bfloat16
VMEM = pl.BlockSpec(memory_space=pltpu.VMEM)


def rows_dot(a, b):
    return lax.dot_general(a, b, (((1,), (1,)), ((), ())), preferred_element_type=F32)


def plain_dot(a, b):
    return lax.dot_general(a, b, (((1,), (0,)), ((), ())), preferred_element_type=F32)


def call(kernel, outs, args, flops=0, exps=0, scratch=()):
    size = sum(a.size * a.dtype.itemsize for a in args)
    return pl.pallas_call(
        kernel,
        out_shape=outs,
        in_specs=[VMEM] * len(args),
        out_specs=jax.tree.map(lambda _: VMEM, outs),
        scratch_shapes=list(scratch),
        compiler_params=pltpu.CompilerParams(vmem_limit_bytes=VMEM_LIMIT),
        cost_estimate=pl.CostEstimate(flops=flops // 64, bytes_accessed=size // 64, transcendentals=0),
    )(*args)


def head_lanes(head):
    return pl.ds(pl.multiple_of(head * HS, HS), HS)


def dead_bias(hist, rows, width):
    count = hist[2 * rows : 2 * rows + 16, 0:HS].astype(F32)[0:1]
    slot = lax.broadcasted_iota(jnp.int32, (rows, HS), 0).astype(F32)
    bias = jnp.where(slot < count, 0.0, LOW)
    return jnp.concatenate([bias] * (width // HS), axis=1)


def flatten(blocks):
    return [a for block in blocks for a in (block if isinstance(block, list) else [block])]


def regroup(refs, blocks):
    refs = list(refs)
    return [[refs.pop(0) for _ in block] if isinstance(block, list) else refs.pop(0) for block in blocks]


def take(block, which, lanes):
    return block[which][:, lanes] if isinstance(block, list) else block[which, :, lanes]


def wide(blocks, which, lanes):
    return jnp.concatenate([take(block, which, lanes) for block in blocks], axis=0)


def stat_step(keys, values, queries, grads, state, bias):
    top, total, dots = state
    scores = rows_dot(keys, queries)
    if bias is not None:
        scores = scores + bias
    new_top = jnp.maximum(top, jnp.max(scores, axis=0, keepdims=True))
    shrink = jnp.exp2((top - new_top) * EXP2_SCALE)
    weights = jnp.exp2((scores - new_top) * EXP2_SCALE)
    grad_scores = rows_dot(values, grads)
    total = total * shrink + jnp.sum(weights, axis=0, keepdims=True)
    dots = dots * shrink + jnp.sum(weights * grad_scores, axis=0, keepdims=True)
    return new_top, total, dots


def stats_call(curs, hists, queries, groups, state_in=None, at=(0, 1, 2, 3)):
    nk, nh, nq = len(flatten(curs)), len(hists), len(flatten(queries))
    rows, feat = hists[0].shape[0] // 2 - 8, hists[0].shape[1]
    tokens = queries[0].shape[1]
    heads = feat // HS

    def kernel(*refs):
        cur, hist = regroup(refs[:nk], curs), refs[nk : nk + nh]
        query = regroup(refs[nk + nh : nk + nh + nq], queries)
        old, out = refs[nk + nh + nq], refs[-1]
        if state_in is not None:
            out[...] = old[...]

        def step(head, _):
            lanes = head_lanes(head)
            for blocks, cur_blocks, hist_blocks, fresh in groups:
                width = tokens * len(blocks)
                asked = wide([query[b] for b in blocks], 0, lanes)
                grads = wide([query[b] for b in blocks], 1, lanes)
                if fresh:
                    state = (
                        jnp.full((1, width), LOW, F32),
                        jnp.zeros((1, width), F32),
                        jnp.zeros((1, width), F32),
                    )
                else:
                    state = tuple(
                        jnp.concatenate(
                            [old[i, pl.ds(head * 4 + at[b], 1), :] for b in blocks], axis=1
                        )
                        for i in range(3)
                    )
                for kb in cur_blocks:
                    state = stat_step(
                        take(cur[kb], 0, lanes), take(cur[kb], 1, lanes), asked, grads, state, None
                    )
                for kb in hist_blocks:
                    state = stat_step(
                        hist[kb][0:rows, lanes],
                        hist[kb][rows : 2 * rows, lanes],
                        asked,
                        grads,
                        state,
                        dead_bias(hist[kb], rows, width),
                    )
                for i in range(3):
                    for j, b in enumerate(blocks):
                        out[i, pl.ds(head * 4 + at[b], 1), :] = state[i][
                            :, j * tokens : (j + 1) * tokens
                        ]
            return 0

        lax.fori_loop(0, heads, step, 0)

    args = flatten(curs) + list(hists) + flatten(queries) + ([] if state_in is None else [state_in])
    work = sum(len(b) * (len(c) + len(h)) for b, c, h, _ in groups) * rows * tokens
    out = jax.ShapeDtypeStruct((3, 16, tokens), F32)
    return call(kernel, out, args, flops=2 * 2 * 2 * work * feat, exps=work * heads)


def combine_stats(stats, base_ref, delta_ref, heads):
    for head in range(heads):
        for block, offset in enumerate(OFFSETS):
            parts = []
            for ref, step in zip(stats, OFFSETS):
                there = [o % 4 for o in OFFSETS].index((offset - step) % 4)
                row = head * 4 + there
                parts.append([ref[i, row : row + 1, :] for i in range(3)])
            top = jnp.maximum(
                jnp.maximum(parts[0][0], parts[1][0]), jnp.maximum(parts[2][0], parts[3][0])
            )
            total = jnp.zeros_like(top)
            dots = jnp.zeros_like(top)
            for part in parts:
                shrink = jnp.exp2((part[0] - top) * EXP2_SCALE)
                total = total + part[1] * shrink
                dots = dots + part[2] * shrink
            at = slice(block * top.shape[1], (block + 1) * top.shape[1])
            base_ref[head, 0:1, at] = top + jnp.log2(total) * (1.0 / EXP2_SCALE)
            delta_ref[head, 0:1, at] = dots / total


def grads_call(curs, hists, queries, stats, sums_in=None, far=None):
    nk, nq = len(curs), len(queries)
    rows, feat = hists[0].shape[0] // 2 - 8, hists[0].shape[1]
    tokens = queries[0].shape[1]
    heads = feat // HS
    width = nq * tokens
    n_cur, n_query = len(flatten(curs)), len(flatten(queries))
    last = far is not None

    def kernel(*refs):
        cur, refs = regroup(refs[:n_cur], curs), refs[n_cur:]
        hist, refs = refs[:nk], refs[nk:]
        query, refs = regroup(refs[:n_query], queries), refs[n_query:]
        stat, refs = refs[:4], refs[4:]
        if sums_in is not None:
            old, refs = refs[0], refs[1:]
        if last:
            far_in, refs = refs[0], refs[1:]
        key_out, sum_out = refs[:nk], refs[nk:-2]
        base, delta = refs[-2:]
        combine_stats(stat, base, delta, heads)

        def part(keys, values, queries, grads, lift, shift, bias):
            scores = rows_dot(keys, queries) - lift
            if bias is not None:
                scores = scores + bias
            prob = jnp.exp2(scores * EXP2_SCALE)
            grad_scores = rows_dot(values, grads)
            score_grad = (prob * (grad_scores - shift)).astype(BF16)
            grad_v = plain_dot(prob.astype(BF16), grads)
            grad_k = plain_dot(score_grad, queries) * SCALE
            return score_grad, grad_k, grad_v

        def store(kb, i, lanes, value):
            if last:
                value = value + far_in[i, :, lanes].astype(F32)
            key_out[kb][i, :, lanes] = value.astype(BF16)

        def step(head, _):
            lanes = head_lanes(head)
            asked, grads = wide(query, 0, lanes), wide(query, 1, lanes)
            lift, shift = base[head, 0:1, :], delta[head, 0:1, :]
            total = None if sums_in is None else old[head]
            for kb in range(nk):
                keys = take(cur[kb], 0, lanes)
                score_a, grad_k, grad_v = part(
                    keys, take(cur[kb], 1, lanes), asked, grads, lift, shift, None
                )
                store(kb, 0, lanes, grad_k)
                store(kb, 1, lanes, grad_v)
                old_keys = hist[kb][0:rows, lanes]
                score_b, grad_k, grad_v = part(
                    old_keys,
                    hist[kb][rows : 2 * rows, lanes],
                    asked,
                    grads,
                    lift,
                    shift,
                    dead_bias(hist[kb], rows, width),
                )
                store(kb, 2, lanes, grad_k)
                store(kb, 3, lanes, grad_v)
                add = plain_dot(
                    jnp.concatenate([keys, old_keys], axis=0).T,
                    jnp.concatenate([score_a, score_b], axis=0),
                )
                total = add if total is None else total + add
            if last:
                for b in range(nq):
                    piece = total[:, b * tokens : (b + 1) * tokens] * SCALE
                    sum_out[b][:, lanes] = piece.T.astype(BF16)
            else:
                sum_out[0][head] = total
            return 0

        lax.fori_loop(0, heads, step, 0)

    block = jax.ShapeDtypeStruct((4, rows, feat), BF16)
    if last:
        sums = [jax.ShapeDtypeStruct((tokens, feat), BF16)] * nq
    else:
        sums = [jax.ShapeDtypeStruct((heads, HS, width), F32)]
    args = flatten(curs) + list(hists) + flatten(queries) + list(stats)
    args += [a for a in (sums_in, far) if a is not None]
    work = nk * 2 * rows * width
    outs = call(
        kernel,
        [block] * nk + sums,
        args,
        flops=2 * 5 * 2 * work * feat,
        exps=work * heads,
        scratch=[pltpu.VMEM((heads, 8, width), F32)] * 2,
    )
    return list(outs[:nk]), list(outs[nk:])


def pack_call(arrays, key_hist, value_hist, hist_len, sizes):
    rows, columns = arrays[0].shape
    nx, nc = sizes[2:]
    old, feat = key_hist.shape
    n = len(arrays)

    def kernel(*refs):
        ins, (key_in, value_in, count), outs = refs[:n], refs[n : n + 3], refs[n + 3 :]
        same, other, hist, held, sem = outs
        copies = [pltpu.make_async_copy(ref, held.at[i], sem.at[i]) for i, ref in enumerate(ins)]
        copies.append(pltpu.make_async_copy(key_in, hist.at[pl.ds(0, old)], sem.at[n]))
        copies.append(pltpu.make_async_copy(value_in, hist.at[pl.ds(old, old)], sem.at[n + 1]))
        for copy in copies:
            copy.start()
        filled = jnp.full((16, feat), count[0], jnp.int32).astype(F32)
        hist[2 * old :, :] = filled.astype(BF16)
        x, core = lax.axis_index("x"), lax.axis_index("c")
        for i in range(n):
            copies[i].wait()
            for j, step in enumerate(X_STEPS):
                for k, out in enumerate((same, other)):
                    part = lax.rem(x + step, nx) * nc + lax.rem(core + k, nc)
                    at = pl.ds(pl.multiple_of(part * feat, feat), feat)
                    out[i // 2, j, i % 2] = held[i, :, at]
        copies[n].wait()
        copies[n + 1].wait()

    shape = jax.ShapeDtypeStruct((n // 2, nx, 2, rows, feat), BF16)
    return pl.pallas_call(
        kernel,
        out_shape=[shape, shape, jax.ShapeDtypeStruct((2 * old + 16, feat), BF16)],
        in_specs=[pl.BlockSpec(memory_space=pl.ANY)] * (n + 2)
        + [pl.BlockSpec(memory_space=pltpu.SMEM)],
        out_specs=[VMEM] * 3,
        scratch_shapes=[
            pltpu.VMEM((n, rows, columns), BF16),
            pltpu.SemaphoreType.DMA((n + 2,)),
        ],
        compiler_params=pltpu.CompilerParams(vmem_limit_bytes=PACK_LIMIT),
    )(*arrays, key_hist, value_hist, hist_len)


def merge_call(same, other):
    pairs, nx, two, rows, feat = same.shape

    def kernel(a, b, *outs):
        for i in range(pairs):
            for j in range(nx):
                outs[i * nx + j][:, 0:rows, :] = a[i, j]
                outs[i * nx + j][:, rows : 2 * rows, :] = b[i, j]

    shape = jax.ShapeDtypeStruct((two, 2 * rows, feat), BF16)
    outs = call(kernel, [shape] * (pairs * nx), [same, other])
    return [list(outs[i * nx : (i + 1) * nx]) for i in range(pairs)]


def stack_call(blocks):
    two, rows, feat = blocks[0].shape

    def kernel(*refs):
        for j, ref in enumerate(refs[:-1]):
            refs[-1][:, j * rows : (j + 1) * rows, :] = ref[...]

    shape = jax.ShapeDtypeStruct((two, len(blocks) * rows, feat), BF16)
    return call(kernel, shape, blocks)


def unpack_call(array, count):
    parts, rows, feat = array.shape
    rows //= count

    def kernel(ref, *outs):
        for i, out in enumerate(outs):
            for p in range(parts):
                out[:, p * feat : (p + 1) * feat] = ref[p, i * rows : (i + 1) * rows, :]

    return call(kernel, [jax.ShapeDtypeStruct((rows, parts * feat), BF16)] * count, [array])


def add_call(query_parts, cur_parts, sizes):
    tokens, feat = query_parts[0].shape
    nx, nc = sizes[2:]
    parts = nx * nc
    rows = tokens // parts
    nq = len(query_parts)

    def kernel(*refs):
        out = refs[-1]
        x, core = lax.axis_index("x"), lax.axis_index("c")
        sums = [
            sum(ref[...].astype(F32) for ref in refs[:nq]),
            sum(ref[0].astype(F32) for ref in refs[nq:-1]),
            sum(ref[1].astype(F32) for ref in refs[nq:-1]),
        ]
        for i, total in enumerate(sums):
            low = total.astype(BF16)
            for j, step in enumerate(X_STEPS):
                for k in range(nc):
                    owner = lax.rem(x + nx - step, nx) * nc + lax.rem(core + k, nc)
                    first = (j * nc + k) * rows
                    out[owner, i * rows : (i + 1) * rows, :] = low[first : first + rows]

    shape = jax.ShapeDtypeStruct((parts, 3 * rows, feat), BF16)
    return call(kernel, shape, list(query_parts) + list(cur_parts))


def add_hist_call(key_parts):
    _, rows, feat = key_parts[0].shape

    def kernel(*refs):
        for i, out in enumerate(refs[-2:]):
            out[...] = sum(ref[2 + i].astype(F32) for ref in refs[:-2]).astype(BF16)

    return call(kernel, [jax.ShapeDtypeStruct((rows, feat), BF16)] * 2, list(key_parts))


def ring_moves(sizes):
    nz, ny, nx, nc = sizes

    def table(target):
        pairs = []
        for z in range(nz):
            for y in range(ny):
                for x in range(nx):
                    for c in range(nc):
                        tz, ty, tx, tc = target(z, y, x, c)
                        src = ((z * ny + y) * nx + x) * nc + c
                        dst = ((tz % nz) * ny + ty % ny) * nx + tx % nx
                        pairs.append((src, dst * nc + tc % nc))
        return pairs

    def keys(step):
        return table(lambda z, y, x, c: (z, y + step, x, c) if c == 0 else (z + step, y, x, c))

    def queries(step):
        return table(lambda z, y, x, c: (z + step, y, x, c) if c == 0 else (z, y + step, x, c))

    def chips(step):
        return table(lambda z, y, x, c: (z, y, x + step, c))

    def cores():
        return table(lambda z, y, x, c: (z, y, x, c + 1))

    return keys, queries, chips, cores


def make_shards(sizes):
    key_move, query_move, chip_move, core_move = ring_moves(sizes)

    def to_key(value, step):
        return lax.ppermute(value, AXES, key_move(step))

    def to_query(value, step):
        return lax.ppermute(value, AXES, query_move(step))

    def shards(query, key_cur, value_cur, d_out, key_hist, value_hist, hist_len):
        same, other, hist0 = pack_call(
            [query, d_out, key_cur, value_cur], key_hist, value_hist, hist_len, sizes
        )
        other = lax.ppermute(other, AXES, core_move())
        hists = [hist0] + [to_key(hist0, -o) for o in OFFSETS[1:]]
        asked, kept = merge_call(same, other)
        kept, hists[1], hists[2] = lax.optimization_barrier((kept, hists[1], hists[2]))

        def exchange(pieces):
            moved = [
                lax.ppermute(p, AXES, chip_move(d)) for p, d in zip(pieces[1:], X_STEPS[1:])
            ]
            return stack_call(pieces[:1] + moved)

        query0 = exchange(asked)
        queries = [query0] + [to_query(query0, -o) for o in OFFSETS[1:]]
        cur0 = exchange(kept)
        curs = [cur0] + [to_key(cur0, -o) for o in OFFSETS[1:]]
        every = (0, 1, 2, 3)
        state = stats_call(
            curs[:1], hists, [queries[0], queries[3]], [((0, 1), (0,), every, True)], at=(0, 3)
        )
        state = stats_call(
            curs[:1], hists, queries[1:3], [((0, 1), (0,), every, True)], state, at=(1, 2)
        )
        state = stats_call(curs, hists[:1], queries, [(every, (1, 2, 3), (), False)], state)
        stats = [state] + [to_query(state, -o) for o in OFFSETS[1:]]

        far, sums = grads_call(curs[3:], hists[3:], queries, stats)
        far = to_key(far[0], 2)
        near, sums = grads_call(curs[1:3], hists[1:3], queries, stats, sums[0])
        near = [to_key(block, offset) for block, offset in zip(near, OFFSETS[1:3])]
        own, sums = grads_call(curs[:1], hists[:1], queries, stats, sums[0], far)
        query_parts = [sums[0]] + [to_query(sums[i], OFFSETS[i]) for i in range(1, 4)]

        back = add_call(query_parts, own + near, sizes)
        back = lax.all_to_all(back, ("x", "c"), 0, 0, tiled=True)
        outs = unpack_call(back, 3)
        grad_k, grad_v = add_hist_call(own + near)
        return outs[0], outs[1], outs[2], grad_k, grad_v

    return shards


def solution(mesh):
    sizes = (4, 4, 4, 2)
    grid = Mesh(mesh.devices.reshape(sizes), AXES)
    token = P(AXES, None)
    hist = P(("z", "y"), ("x", "c"))
    return jax.shard_map(
        make_shards(sizes),
        mesh=grid,
        in_specs=(token, token, token, token, hist, hist, P(("z", "y"))),
        out_specs=(token, token, token, hist, hist),
        check_vma=False,
    )
```

```python
import math

import jax
import jax.numpy as jnp
from jax import lax
from jax.experimental import pallas as pl
from jax.experimental.pallas import tpu as pltpu
from jax.sharding import Mesh
from jax.sharding import PartitionSpec as P

HS = 128
SCALE = 1.0 / math.sqrt(HS)
EXP2_SCALE = SCALE * math.log2(math.e)
LOW = -1e30
VMEM_LIMIT = 12 * 1024 * 1024
PACK_LIMIT = 56 * 1024 * 1024
SAVED = (0, 1, 4)
AXES = ("z", "y", "x", "c")
OFFSETS = (0, -1, 1, 2)
X_STEPS = (0, 1, 3, 2)
F32 = jnp.float32
BF16 = jnp.bfloat16
VMEM = pl.BlockSpec(memory_space=pltpu.VMEM)


def rows_dot(a, b):
    return lax.dot_general(a, b, (((1,), (1,)), ((), ())), preferred_element_type=F32)


def plain_dot(a, b):
    return lax.dot_general(a, b, (((1,), (0,)), ((), ())), preferred_element_type=F32)


def call(kernel, outs, args, flops=0, exps=0, scratch=()):
    size = sum(a.size * a.dtype.itemsize for a in args)
    return pl.pallas_call(
        kernel,
        out_shape=outs,
        in_specs=[VMEM] * len(args),
        out_specs=jax.tree.map(lambda _: VMEM, outs),
        scratch_shapes=list(scratch),
        compiler_params=pltpu.CompilerParams(vmem_limit_bytes=VMEM_LIMIT),
        cost_estimate=pl.CostEstimate(flops=flops // 64, bytes_accessed=size // 64, transcendentals=0),
    )(*args)


def head_lanes(head):
    return pl.ds(pl.multiple_of(head * HS, HS), HS)


def dead_bias(hist, rows, width):
    count = hist[2 * rows : 2 * rows + 16, 0:HS].astype(F32)[0:1]
    slot = lax.broadcasted_iota(jnp.int32, (rows, HS), 0).astype(F32)
    bias = jnp.where(slot < count, 0.0, LOW)
    return jnp.concatenate([bias] * (width // HS), axis=1)


def wide(blocks, which, lanes):
    return jnp.concatenate([block[which, :, lanes] for block in blocks], axis=0)


def stat_step(keys, values, queries, grads, state, bias, keep):
    top, total, dots = state
    scores = rows_dot(keys, queries)
    if bias is not None:
        scores = scores + bias
    new_top = jnp.maximum(top, jnp.max(scores, axis=0, keepdims=True))
    shrink = jnp.exp2((top - new_top) * EXP2_SCALE)
    weights = jnp.exp2((scores - new_top) * EXP2_SCALE)
    grad_scores = rows_dot(values, grads)
    total = total * shrink + jnp.sum(weights, axis=0, keepdims=True)
    dots = dots * shrink + jnp.sum(weights * grad_scores, axis=0, keepdims=True)
    if keep is not None:
        keep(scores, grad_scores)
    return new_top, total, dots


def stats_call(curs, hists, queries, at, state_in=None, fresh=True, saved=()):
    nk, nh, nq = len(curs), len(hists), len(queries)
    tokens, feat = queries[0].shape[1:]
    rows = tokens
    heads = feat // HS
    width = tokens * nq

    def kernel(*refs):
        cur, refs = refs[:nk], refs[nk:]
        hist, refs = refs[:nh], refs[nh:]
        query, refs = refs[:nq], refs[nq:]
        if state_in is not None:
            old, refs = refs[0], refs[1:]
        out, tiles = refs[0], refs[1:]
        if state_in is not None:
            out[...] = old[...]

        def step(head, _):
            lanes = head_lanes(head)
            asked, grads = wide(query, 0, lanes), wide(query, 1, lanes)
            places = [pl.ds(head * 4 + b, 1) for b in at]
            if fresh:
                low, zero = jnp.full((1, width), LOW, F32), jnp.zeros((1, width), F32)
                state = (low, zero, zero)
            else:
                state = tuple(
                    jnp.concatenate([old[i, row, :] for row in places], axis=1) for i in range(3)
                )

            def keep_of(block):
                if block not in saved:
                    return None
                i = saved.index(block)

                def keep(scores, grad_scores):
                    tiles[2 * i][head] = scores
                    tiles[2 * i + 1][head] = grad_scores

                return keep

            for i in range(nk):
                keys, values = cur[i][0, :, lanes], cur[i][1, :, lanes]
                state = stat_step(keys, values, asked, grads, state, None, keep_of(i))
            for i in range(nh):
                keys, values = hist[i][0:rows, lanes], hist[i][rows : 2 * rows, lanes]
                bias = dead_bias(hist[i], rows, width)
                state = stat_step(keys, values, asked, grads, state, bias, keep_of(nk + i))
            for i in range(3):
                for j, row in enumerate(places):
                    out[i, row, :] = state[i][:, j * tokens : (j + 1) * tokens]
            return 0

        lax.fori_loop(0, heads, step, 0)

    args = list(curs) + list(hists) + list(queries) + ([] if state_in is None else [state_in])
    work = (nk + nh) * rows * width
    outs = [jax.ShapeDtypeStruct((3, 16, tokens), F32)]
    outs += [jax.ShapeDtypeStruct((heads, rows, width), F32)] * (2 * len(saved))
    outs = call(kernel, outs, args, flops=2 * 2 * 2 * work * feat, exps=work * heads)
    return outs[0], [tuple(outs[1 + 2 * i : 3 + 2 * i]) for i in range(len(saved))]


def combine_stats(stats, base_ref, delta_ref, heads):
    for head in range(heads):
        for block, offset in enumerate(OFFSETS):
            parts = []
            for ref, step in zip(stats, OFFSETS):
                there = [o % 4 for o in OFFSETS].index((offset - step) % 4)
                row = head * 4 + there
                parts.append([ref[i, row : row + 1, :] for i in range(3)])
            top = jnp.maximum(
                jnp.maximum(parts[0][0], parts[1][0]), jnp.maximum(parts[2][0], parts[3][0])
            )
            total = jnp.zeros_like(top)
            dots = jnp.zeros_like(top)
            for part in parts:
                shrink = jnp.exp2((part[0] - top) * EXP2_SCALE)
                total = total + part[1] * shrink
                dots = dots + part[2] * shrink
            at = slice(block * top.shape[1], (block + 1) * top.shape[1])
            base_ref[head, 0:1, at] = top + jnp.log2(total) * (1.0 / EXP2_SCALE)
            delta_ref[head, 0:1, at] = dots / total


def grads_call(curs, hists, queries, stats, tiles, sums_in=None, far=None):
    nk, nq = len(curs), len(queries)
    tokens, feat = queries[0].shape[1:]
    rows = tokens
    heads = feat // HS
    width = nq * tokens
    last = far is not None
    held = [a for pieces in tiles.values() for pair, _ in pieces for a in pair]

    def kernel(*refs):
        cur, refs = refs[:nk], refs[nk:]
        hist, refs = refs[:nk], refs[nk:]
        query, refs = refs[:nq], refs[nq:]
        stat, refs = refs[:4], refs[4:]
        held_refs, refs = list(refs[: len(held)]), refs[len(held) :]
        found = {
            block: [(held_refs.pop(0), held_refs.pop(0), blocks) for _, blocks in pieces]
            for block, pieces in tiles.items()
        }
        if sums_in is not None:
            old, refs = refs[0], refs[1:]
        if last:
            far_in, refs = refs[0], refs[1:]
        key_out, sum_out = refs[:nk], refs[nk:-2]
        base, delta = refs[-2:]
        combine_stats(stat, base, delta, heads)

        def saved_tile(block, which, head):
            parts = {}
            for *pair, blocks in found[block]:
                for j, b in enumerate(blocks):
                    parts[b] = pair[which][head, :, j * tokens : (j + 1) * tokens]
            return jnp.concatenate([parts[b] for b in range(nq)], axis=1)

        def part(block, head, keys, values, asked, grads, lift, shift, bias):
            if block in found:
                scores, grad_scores = saved_tile(block, 0, head), saved_tile(block, 1, head)
            else:
                scores, grad_scores = rows_dot(keys, asked), rows_dot(values, grads)
                if bias is not None:
                    scores = scores + bias
            prob = jnp.exp2((scores - lift) * EXP2_SCALE)
            score_grad = (prob * (grad_scores - shift)).astype(BF16)
            grad_v = plain_dot(prob.astype(BF16), grads)
            grad_k = plain_dot(score_grad, asked) * SCALE
            return score_grad, (grad_k, grad_v)

        def step(head, _):
            lanes = head_lanes(head)
            asked, grads = wide(query, 0, lanes), wide(query, 1, lanes)
            lift, shift = base[head, 0:1, :], delta[head, 0:1, :]
            total = None if sums_in is None else old[head]
            for kb in range(nk):
                blocks = [
                    (cur[kb][0, :, lanes], cur[kb][1, :, lanes], None),
                    (
                        hist[kb][0:rows, lanes],
                        hist[kb][rows : 2 * rows, lanes],
                        dead_bias(hist[kb], rows, width),
                    ),
                ]
                all_scores = []
                for i, (keys, values, bias) in enumerate(blocks):
                    score_grad, both = part(
                        2 * kb + i, head, keys, values, asked, grads, lift, shift, bias
                    )
                    all_scores.append(score_grad)
                    for j in range(2):
                        value = both[j]
                        if last:
                            value = value + far_in[2 * i + j, :, lanes].astype(F32)
                        key_out[kb][2 * i + j, :, lanes] = value.astype(BF16)
                add = plain_dot(
                    jnp.concatenate([keys for keys, _, _ in blocks], axis=0).T,
                    jnp.concatenate(all_scores, axis=0),
                )
                total = add if total is None else total + add
            if last:
                for b in range(nq):
                    piece = total[:, b * tokens : (b + 1) * tokens] * SCALE
                    sum_out[b][:, lanes] = piece.T.astype(BF16)
            else:
                sum_out[0][head] = total
            return 0

        lax.fori_loop(0, heads, step, 0)

    block = jax.ShapeDtypeStruct((4, rows, feat), BF16)
    if last:
        sums = [jax.ShapeDtypeStruct((tokens, feat), BF16)] * nq
    else:
        sums = [jax.ShapeDtypeStruct((heads, HS, width), F32)]
    args = list(curs) + list(hists) + list(queries) + list(stats) + held
    args += [a for a in (sums_in, far) if a is not None]
    work = nk * 2 * rows * width
    outs = call(
        kernel,
        [block] * nk + sums,
        args,
        flops=2 * 5 * 2 * work * feat,
        exps=work * heads,
        scratch=[pltpu.VMEM((heads, 8, width), F32)] * 2,
    )
    return list(outs[:nk]), list(outs[nk:])


def pack_call(arrays, key_hist, value_hist, hist_len, sizes):
    rows, columns = arrays[0].shape
    nx, nc = sizes[2:]
    old, feat = key_hist.shape
    n = len(arrays)

    def kernel(*refs):
        ins, (key_in, value_in, count), outs = refs[:n], refs[n : n + 3], refs[n + 3 :]
        same, other, hist, held, sem = outs
        copies = [pltpu.make_async_copy(ref, held.at[i], sem.at[i]) for i, ref in enumerate(ins)]
        copies.append(pltpu.make_async_copy(key_in, hist.at[pl.ds(0, old)], sem.at[n]))
        copies.append(pltpu.make_async_copy(value_in, hist.at[pl.ds(old, old)], sem.at[n + 1]))
        for copy in copies:
            copy.start()
        filled = jnp.full((16, feat), count[0], jnp.int32).astype(F32)
        hist[2 * old :, :] = filled.astype(BF16)
        x, core = lax.axis_index("x"), lax.axis_index("c")
        for i in range(n):
            copies[i].wait()
            for j, step in enumerate(X_STEPS):
                for k, out in enumerate((same, other)):
                    part = lax.rem(x + step, nx) * nc + lax.rem(core + k, nc)
                    at = pl.ds(pl.multiple_of(part * feat, feat), feat)
                    out[i // 2, j, i % 2] = held[i, :, at]
        copies[n].wait()
        copies[n + 1].wait()

    shape = jax.ShapeDtypeStruct((n // 2, nx, 2, rows, feat), BF16)
    return pl.pallas_call(
        kernel,
        out_shape=[shape, shape, jax.ShapeDtypeStruct((2 * old + 16, feat), BF16)],
        in_specs=[pl.BlockSpec(memory_space=pl.ANY)] * (n + 2)
        + [pl.BlockSpec(memory_space=pltpu.SMEM)],
        out_specs=[VMEM] * 3,
        scratch_shapes=[
            pltpu.VMEM((n, rows, columns), BF16),
            pltpu.SemaphoreType.DMA((n + 2,)),
        ],
        compiler_params=pltpu.CompilerParams(vmem_limit_bytes=PACK_LIMIT),
    )(*arrays, key_hist, value_hist, hist_len)


def merge_call(same, other):
    pairs, nx, two, rows, feat = same.shape

    def kernel(a, b, *outs):
        for i in range(pairs):
            for j in range(nx):
                outs[i * nx + j][:, 0:rows, :] = a[i, j]
                outs[i * nx + j][:, rows : 2 * rows, :] = b[i, j]

    shape = jax.ShapeDtypeStruct((two, 2 * rows, feat), BF16)
    outs = call(kernel, [shape] * (pairs * nx), [same, other])
    return [list(outs[i * nx : (i + 1) * nx]) for i in range(pairs)]


def stack_call(blocks):
    two, rows, feat = blocks[0].shape

    def kernel(*refs):
        for j, ref in enumerate(refs[:-1]):
            refs[-1][:, j * rows : (j + 1) * rows, :] = ref[...]

    shape = jax.ShapeDtypeStruct((two, len(blocks) * rows, feat), BF16)
    return call(kernel, shape, blocks)


def unpack_call(array, count):
    parts, rows, feat = array.shape
    rows //= count

    def kernel(ref, *outs):
        for i, out in enumerate(outs):
            for p in range(parts):
                out[:, p * feat : (p + 1) * feat] = ref[p, i * rows : (i + 1) * rows, :]

    return call(kernel, [jax.ShapeDtypeStruct((rows, parts * feat), BF16)] * count, [array])


def add_call(query_parts, cur_parts, sizes):
    tokens, feat = query_parts[0].shape
    nx, nc = sizes[2:]
    parts = nx * nc
    rows = tokens // parts
    nq = len(query_parts)

    def kernel(*refs):
        out = refs[-1]
        x, core = lax.axis_index("x"), lax.axis_index("c")
        sums = [
            sum(ref[...].astype(F32) for ref in refs[:nq]),
            sum(ref[0].astype(F32) for ref in refs[nq:-1]),
            sum(ref[1].astype(F32) for ref in refs[nq:-1]),
        ]
        for i, total in enumerate(sums):
            low = total.astype(BF16)
            for j, step in enumerate(X_STEPS):
                for k in range(nc):
                    owner = lax.rem(x + nx - step, nx) * nc + lax.rem(core + k, nc)
                    first = (j * nc + k) * rows
                    out[owner, i * rows : (i + 1) * rows, :] = low[first : first + rows]

    shape = jax.ShapeDtypeStruct((parts, 3 * rows, feat), BF16)
    return call(kernel, shape, list(query_parts) + list(cur_parts))


def add_hist_call(key_parts):
    _, rows, feat = key_parts[0].shape

    def kernel(*refs):
        for i, out in enumerate(refs[-2:]):
            out[...] = sum(ref[2 + i].astype(F32) for ref in refs[:-2]).astype(BF16)

    return call(kernel, [jax.ShapeDtypeStruct((rows, feat), BF16)] * 2, list(key_parts))


def ring_moves(sizes):
    nz, ny, nx, nc = sizes

    def table(target):
        pairs = []
        for z in range(nz):
            for y in range(ny):
                for x in range(nx):
                    for c in range(nc):
                        tz, ty, tx, tc = target(z, y, x, c)
                        src = ((z * ny + y) * nx + x) * nc + c
                        dst = ((tz % nz) * ny + ty % ny) * nx + tx % nx
                        pairs.append((src, dst * nc + tc % nc))
        return pairs

    def keys(step):
        return table(lambda z, y, x, c: (z, y + step, x, c) if c == 0 else (z + step, y, x, c))

    def queries(step):
        return table(lambda z, y, x, c: (z + step, y, x, c) if c == 0 else (z, y + step, x, c))

    def chips(step):
        return table(lambda z, y, x, c: (z, y, x + step, c))

    def cores():
        return table(lambda z, y, x, c: (z, y, x, c + 1))

    return keys, queries, chips, cores


def make_shards(sizes):
    key_move, query_move, chip_move, core_move = ring_moves(sizes)

    def to_key(value, step):
        return lax.ppermute(value, AXES, key_move(step))

    def to_query(value, step):
        return lax.ppermute(value, AXES, query_move(step))

    def shards(query, key_cur, value_cur, d_out, key_hist, value_hist, hist_len):
        same, other, hist0 = pack_call(
            [query, d_out, key_cur, value_cur], key_hist, value_hist, hist_len, sizes
        )
        other = lax.ppermute(other, AXES, core_move())
        hists = [hist0] + [to_key(hist0, -o) for o in OFFSETS[1:]]
        asked, kept = merge_call(same, other)
        kept, hists[1], hists[2] = lax.optimization_barrier((kept, hists[1], hists[2]))

        def exchange(pieces):
            moved = [
                lax.ppermute(p, AXES, chip_move(d)) for p, d in zip(pieces[1:], X_STEPS[1:])
            ]
            return stack_call(pieces[:1] + moved)

        query0 = exchange(asked)
        queries = [query0] + [to_query(query0, -o) for o in OFFSETS[1:]]
        cur0 = exchange(kept)
        curs = [cur0] + [to_key(cur0, -o) for o in OFFSETS[1:]]
        every = (0, 1, 2, 3)
        ends, middle = (0, 3), (1, 2)
        state, kept_a = stats_call(
            curs[:1], hists, [queries[0], queries[3]], ends, saved=SAVED
        )
        state, kept_b = stats_call(curs[:1], hists, queries[1:3], middle, state, saved=SAVED)
        state, kept_c = stats_call(
            curs[1:], [], queries, every, state, fresh=False, saved=(0, 1, 2)
        )
        stats = [state] + [to_query(state, -o) for o in OFFSETS[1:]]
        held = {("cur", 1 + i): [(pair, every)] for i, pair in enumerate(kept_c)}
        for i, a, b in zip(SAVED, kept_a, kept_b):
            name = ("hist", i - 1) if i else ("cur", 0)
            held[name] = [(a, ends), (b, middle)]

        def tiles(*blocks):
            names = [(kind, b) for b in blocks for kind in ("cur", "hist")]
            return {i: held[name] for i, name in enumerate(names) if name in held}

        far, sums = grads_call(curs[3:], hists[3:], queries, stats, tiles(3))
        far = to_key(far[0], 2)
        near, sums = grads_call(curs[1:3], hists[1:3], queries, stats, tiles(1, 2), sums[0])
        near = [to_key(block, offset) for block, offset in zip(near, OFFSETS[1:3])]
        own, sums = grads_call(curs[:1], hists[:1], queries, stats, tiles(0), sums[0], far)
        query_parts = [sums[0]] + [to_query(sums[i], OFFSETS[i]) for i in range(1, 4)]

        back = add_call(query_parts, own + near, sizes)
        back = lax.all_to_all(back, ("x", "c"), 0, 0, tiled=True)
        outs = unpack_call(back, 3)
        grad_k, grad_v = add_hist_call(own + near)
        return outs[0], outs[1], outs[2], grad_k, grad_v

    return shards


def solution(mesh):
    sizes = (4, 4, 4, 2)
    grid = Mesh(mesh.devices.reshape(sizes), AXES)
    token = P(AXES, None)
    hist = P(("z", "y"), ("x", "c"))
    return jax.shard_map(
        make_shards(sizes),
        mesh=grid,
        in_specs=(token, token, token, token, hist, hist, P(("z", "y"))),
        out_specs=(token, token, token, hist, hist),
        check_vma=False,
    )
```

```python
import math

import jax
import jax.numpy as jnp
from jax import lax
from jax.experimental import pallas as pl
from jax.experimental.pallas import tpu as pltpu
from jax.sharding import Mesh
from jax.sharding import PartitionSpec as P

HS = 128
SCALE = 1.0 / math.sqrt(HS)
EXP2_SCALE = SCALE * math.log2(math.e)
LOW = -1e30
VMEM_LIMIT = 12 * 1024 * 1024
PACK_LIMIT = 56 * 1024 * 1024
SAVED = (0, 1, 4)
AXES = ("z", "y", "x", "c")
OFFSETS = (0, -1, 1, 2)
X_STEPS = (0, 1, 3, 2)
F32 = jnp.float32
BF16 = jnp.bfloat16
VMEM = pl.BlockSpec(memory_space=pltpu.VMEM)


def rows_dot(a, b):
    return lax.dot_general(a, b, (((1,), (1,)), ((), ())), preferred_element_type=F32)


def plain_dot(a, b):
    return lax.dot_general(a, b, (((1,), (0,)), ((), ())), preferred_element_type=F32)


def call(kernel, outs, args, flops=0, exps=0, scratch=()):
    size = sum(a.size * a.dtype.itemsize for a in args)
    return pl.pallas_call(
        kernel,
        out_shape=outs,
        in_specs=[VMEM] * len(args),
        out_specs=jax.tree.map(lambda _: VMEM, outs),
        scratch_shapes=list(scratch),
        compiler_params=pltpu.CompilerParams(vmem_limit_bytes=VMEM_LIMIT),
        cost_estimate=pl.CostEstimate(flops=flops // 64, bytes_accessed=size // 64, transcendentals=0),
    )(*args)


def head_lanes(head):
    return pl.ds(pl.multiple_of(head * HS, HS), HS)


def dead_bias(hist, rows, width):
    count = hist[2 * rows : 2 * rows + 16, 0:HS].astype(F32)[0:1]
    slot = lax.broadcasted_iota(jnp.int32, (rows, HS), 0).astype(F32)
    bias = jnp.where(slot < count, 0.0, LOW)
    return jnp.concatenate([bias] * (width // HS), axis=1)


def wide(blocks, which, lanes):
    return jnp.concatenate([block[which, :, lanes] for block in blocks], axis=0)


def stat_step(keys, values, queries, grads, state, bias, keep):
    top, total, dots = state
    scores = rows_dot(keys, queries)
    if bias is not None:
        scores = scores + bias
    new_top = jnp.maximum(top, jnp.max(scores, axis=0, keepdims=True))
    shrink = jnp.exp2((top - new_top) * EXP2_SCALE)
    weights = jnp.exp2((scores - new_top) * EXP2_SCALE)
    grad_scores = rows_dot(values, grads)
    total = total * shrink + jnp.sum(weights, axis=0, keepdims=True)
    dots = dots * shrink + jnp.sum(weights * grad_scores, axis=0, keepdims=True)
    if keep is not None:
        keep(scores, grad_scores)
    return new_top, total, dots


def stats_call(curs, hists, queries, at, state_in=None, fresh=True, saved=()):
    nk, nh, nq = len(curs), len(hists), len(queries)
    tokens, feat = queries[0].shape[1:]
    rows = tokens
    heads = feat // HS
    width = tokens * nq

    def kernel(*refs):
        cur, refs = refs[:nk], refs[nk:]
        hist, refs = refs[:nh], refs[nh:]
        query, refs = refs[:nq], refs[nq:]
        if state_in is not None:
            old, refs = refs[0], refs[1:]
        out, tiles = refs[0], refs[1:]
        if state_in is not None:
            out[...] = old[...]

        def step(head, _):
            lanes = head_lanes(head)
            asked, grads = wide(query, 0, lanes), wide(query, 1, lanes)
            places = [pl.ds(head * 4 + b, 1) for b in at]
            if fresh:
                low, zero = jnp.full((1, width), LOW, F32), jnp.zeros((1, width), F32)
                state = (low, zero, zero)
            else:
                state = tuple(
                    jnp.concatenate([old[i, row, :] for row in places], axis=1) for i in range(3)
                )

            def keep_of(block):
                if block not in saved:
                    return None
                i = saved.index(block)

                def keep(scores, grad_scores):
                    tiles[2 * i][head] = scores
                    tiles[2 * i + 1][head] = grad_scores

                return keep

            for i in range(nk):
                keys, values = cur[i][0, :, lanes], cur[i][1, :, lanes]
                state = stat_step(keys, values, asked, grads, state, None, keep_of(i))
            for i in range(nh):
                keys, values = hist[i][0:rows, lanes], hist[i][rows : 2 * rows, lanes]
                bias = dead_bias(hist[i], rows, width)
                state = stat_step(keys, values, asked, grads, state, bias, keep_of(nk + i))
            for i in range(3):
                for j, row in enumerate(places):
                    out[i, row, :] = state[i][:, j * tokens : (j + 1) * tokens]
            return 0

        lax.fori_loop(0, heads, step, 0)

    args = list(curs) + list(hists) + list(queries) + ([] if state_in is None else [state_in])
    work = (nk + nh) * rows * width
    outs = [jax.ShapeDtypeStruct((3, 16, tokens), F32)]
    outs += [jax.ShapeDtypeStruct((heads, rows, width), F32)] * (2 * len(saved))
    outs = call(kernel, outs, args, flops=2 * 2 * 2 * work * feat, exps=work * heads)
    return outs[0], [tuple(outs[1 + 2 * i : 3 + 2 * i]) for i in range(len(saved))]


def combine_stats(stats, base_ref, delta_ref, heads):
    for head in range(heads):
        for block, offset in enumerate(OFFSETS):
            parts = []
            for ref, step in zip(stats, OFFSETS):
                there = [o % 4 for o in OFFSETS].index((offset - step) % 4)
                row = head * 4 + there
                parts.append([ref[i, row : row + 1, :] for i in range(3)])
            top = jnp.maximum(
                jnp.maximum(parts[0][0], parts[1][0]), jnp.maximum(parts[2][0], parts[3][0])
            )
            total = jnp.zeros_like(top)
            dots = jnp.zeros_like(top)
            for part in parts:
                shrink = jnp.exp2((part[0] - top) * EXP2_SCALE)
                total = total + part[1] * shrink
                dots = dots + part[2] * shrink
            at = slice(block * top.shape[1], (block + 1) * top.shape[1])
            base_ref[head, 0:1, at] = top + jnp.log2(total) * (1.0 / EXP2_SCALE)
            delta_ref[head, 0:1, at] = dots / total


def grads_call(curs, hists, queries, stats, tiles, sums_in=None, last=False, whole=()):
    nk, nq = len(curs), len(queries)
    tokens, feat = queries[0].shape[1:]
    rows = tokens
    heads = feat // HS
    width = nq * tokens
    held = [a for pieces in tiles.values() for pair, _ in pieces for a in pair]

    def kernel(*refs):
        cur, refs = refs[:nk], refs[nk:]
        hist, refs = refs[:nk], refs[nk:]
        query, refs = refs[:nq], refs[nq:]
        stat, refs = refs[:4], refs[4:]
        held_refs, refs = list(refs[: len(held)]), refs[len(held) :]
        found = {
            block: [(held_refs.pop(0), held_refs.pop(0), blocks) for _, blocks in pieces]
            for block, pieces in tiles.items()
        }
        if sums_in is not None:
            old, refs = refs[0], refs[1:]
        key_out, sum_out = refs[:n_out], refs[n_out:-2]
        base, delta = refs[-2:]
        combine_stats(stat, base, delta, heads)

        def saved_tile(block, which, head):
            parts = {}
            for *pair, blocks in found[block]:
                for j, b in enumerate(blocks):
                    parts[b] = pair[which][head, :, j * tokens : (j + 1) * tokens]
            return jnp.concatenate([parts[b] for b in range(nq)], axis=1)

        def part(block, head, keys, values, asked, grads, lift, shift, bias):
            if block in found:
                scores, grad_scores = saved_tile(block, 0, head), saved_tile(block, 1, head)
            else:
                scores, grad_scores = rows_dot(keys, asked), rows_dot(values, grads)
                if bias is not None:
                    scores = scores + bias
            prob = jnp.exp2((scores - lift) * EXP2_SCALE)
            score_grad = (prob * (grad_scores - shift)).astype(BF16)
            grad_v = plain_dot(prob.astype(BF16), grads)
            grad_k = plain_dot(score_grad, asked) * SCALE
            return score_grad, (grad_k, grad_v)

        def step(head, _):
            lanes = head_lanes(head)
            asked, grads = wide(query, 0, lanes), wide(query, 1, lanes)
            lift, shift = base[head, 0:1, :], delta[head, 0:1, :]
            total = None if sums_in is None else old[head]
            for kb in range(nk):
                blocks = [
                    (cur[kb][0, :, lanes], cur[kb][1, :, lanes], None),
                    (
                        hist[kb][0:rows, lanes],
                        hist[kb][rows : 2 * rows, lanes],
                        dead_bias(hist[kb], rows, width),
                    ),
                ]
                all_scores = []
                for i, (keys, values, bias) in enumerate(blocks):
                    score_grad, both = part(
                        2 * kb + i, head, keys, values, asked, grads, lift, shift, bias
                    )
                    all_scores.append(score_grad)
                    for j in range(2):
                        at = firsts[kb]
                        if kb in whole:
                            key_out[at][2 * i + j, :, lanes] = both[j].astype(BF16)
                        else:
                            key_out[at + i][j, :, lanes] = both[j].astype(BF16)
                add = plain_dot(
                    jnp.concatenate([keys for keys, _, _ in blocks], axis=0).T,
                    jnp.concatenate(all_scores, axis=0),
                )
                total = add if total is None else total + add
            if last:
                for b in range(nq):
                    piece = total[:, b * tokens : (b + 1) * tokens] * SCALE
                    sum_out[b][:, lanes] = piece.T.astype(BF16)
            else:
                sum_out[0][head] = total
            return 0

        lax.fori_loop(0, heads, step, 0)

    blocks, firsts = [], []
    for kb in range(nk):
        firsts.append(len(blocks))
        if kb in whole:
            blocks.append(jax.ShapeDtypeStruct((4, rows, feat), BF16))
        else:
            blocks += [jax.ShapeDtypeStruct((2, rows, feat), BF16)] * 2
    n_out = len(blocks)
    if last:
        sums = [jax.ShapeDtypeStruct((tokens, feat), BF16)] * nq
    else:
        sums = [jax.ShapeDtypeStruct((heads, HS, width), F32)]
    args = list(curs) + list(hists) + list(queries) + list(stats) + held
    if sums_in is not None:
        args.append(sums_in)
    work = nk * 2 * rows * width
    outs = call(
        kernel,
        blocks + sums,
        args,
        flops=2 * 5 * 2 * work * feat,
        exps=work * heads,
        scratch=[pltpu.VMEM((heads, 8, width), F32)] * 2,
    )
    return list(outs[:n_out]), list(outs[n_out:])


def pack_call(arrays, key_hist, value_hist, hist_len, sizes):
    rows, columns = arrays[0].shape
    nx, nc = sizes[2:]
    old, feat = key_hist.shape
    n = len(arrays)

    def kernel(*refs):
        ins, (key_in, value_in, count), outs = refs[:n], refs[n : n + 3], refs[n + 3 :]
        same, other, hist, held, sem = outs
        copies = [pltpu.make_async_copy(ref, held.at[i], sem.at[i]) for i, ref in enumerate(ins)]
        copies.append(pltpu.make_async_copy(key_in, hist.at[pl.ds(0, old)], sem.at[n]))
        copies.append(pltpu.make_async_copy(value_in, hist.at[pl.ds(old, old)], sem.at[n + 1]))
        for copy in copies:
            copy.start()
        filled = jnp.full((16, feat), count[0], jnp.int32).astype(F32)
        hist[2 * old :, :] = filled.astype(BF16)
        x, core = lax.axis_index("x"), lax.axis_index("c")
        for i in range(n):
            copies[i].wait()
            for j, step in enumerate(X_STEPS):
                for k, out in enumerate((same, other)):
                    part = lax.rem(x + step, nx) * nc + lax.rem(core + k, nc)
                    at = pl.ds(pl.multiple_of(part * feat, feat), feat)
                    out[i // 2, j, i % 2] = held[i, :, at]
        copies[n].wait()
        copies[n + 1].wait()

    shape = jax.ShapeDtypeStruct((n // 2, nx, 2, rows, feat), BF16)
    return pl.pallas_call(
        kernel,
        out_shape=[shape, shape, jax.ShapeDtypeStruct((2 * old + 16, feat), BF16)],
        in_specs=[pl.BlockSpec(memory_space=pl.ANY)] * (n + 2)
        + [pl.BlockSpec(memory_space=pltpu.SMEM)],
        out_specs=[VMEM] * 3,
        scratch_shapes=[
            pltpu.VMEM((n, rows, columns), BF16),
            pltpu.SemaphoreType.DMA((n + 2,)),
        ],
        compiler_params=pltpu.CompilerParams(vmem_limit_bytes=PACK_LIMIT),
    )(*arrays, key_hist, value_hist, hist_len)


def merge_call(same, other):
    pairs, nx, two, rows, feat = same.shape

    def kernel(a, b, *outs):
        for i in range(pairs):
            for j in range(nx):
                outs[i * nx + j][:, 0:rows, :] = a[i, j]
                outs[i * nx + j][:, rows : 2 * rows, :] = b[i, j]

    shape = jax.ShapeDtypeStruct((two, 2 * rows, feat), BF16)
    outs = call(kernel, [shape] * (pairs * nx), [same, other])
    return [list(outs[i * nx : (i + 1) * nx]) for i in range(pairs)]


def stack_call(blocks):
    two, rows, feat = blocks[0].shape

    def kernel(*refs):
        for j, ref in enumerate(refs[:-1]):
            refs[-1][:, j * rows : (j + 1) * rows, :] = ref[...]

    shape = jax.ShapeDtypeStruct((two, len(blocks) * rows, feat), BF16)
    return call(kernel, shape, blocks)


def unpack_call(array, count):
    parts, rows, feat = array.shape
    rows //= count

    def kernel(ref, *outs):
        for i, out in enumerate(outs):
            for p in range(parts):
                out[:, p * feat : (p + 1) * feat] = ref[p, i * rows : (i + 1) * rows, :]

    return call(kernel, [jax.ShapeDtypeStruct((rows, parts * feat), BF16)] * count, [array])


def add_call(query_parts, cur_parts, sizes):
    tokens, feat = query_parts[0].shape
    nx, nc = sizes[2:]
    parts = nx * nc
    rows = tokens // parts
    nq = len(query_parts)

    def kernel(*refs):
        out = refs[-1]
        x, core = lax.axis_index("x"), lax.axis_index("c")
        sums = [
            sum(ref[...].astype(F32) for ref in refs[:nq]),
            sum(ref[0].astype(F32) for ref in refs[nq:-1]),
            sum(ref[1].astype(F32) for ref in refs[nq:-1]),
        ]
        for i, total in enumerate(sums):
            low = total.astype(BF16)
            for j, step in enumerate(X_STEPS):
                for k in range(nc):
                    owner = lax.rem(x + nx - step, nx) * nc + lax.rem(core + k, nc)
                    first = (j * nc + k) * rows
                    out[owner, i * rows : (i + 1) * rows, :] = low[first : first + rows]

    shape = jax.ShapeDtypeStruct((parts, 3 * rows, feat), BF16)
    return call(kernel, shape, list(query_parts) + list(cur_parts))


def add_hist_call(parts, whole):
    _, rows, feat = parts[0].shape
    n = len(parts)

    def kernel(*refs):
        for i, out in enumerate(refs[-2:]):
            total = sum(ref[i].astype(F32) for ref in refs[:n])
            total = total + sum(ref[2 + i].astype(F32) for ref in refs[n:-2])
            out[...] = total.astype(BF16)

    return call(kernel, [jax.ShapeDtypeStruct((rows, feat), BF16)] * 2, [*parts, *whole])


def ring_moves(sizes):
    nz, ny, nx, nc = sizes

    def table(target):
        pairs = []
        for z in range(nz):
            for y in range(ny):
                for x in range(nx):
                    for c in range(nc):
                        tz, ty, tx, tc = target(z, y, x, c)
                        src = ((z * ny + y) * nx + x) * nc + c
                        dst = ((tz % nz) * ny + ty % ny) * nx + tx % nx
                        pairs.append((src, dst * nc + tc % nc))
        return pairs

    def keys(step):
        return table(lambda z, y, x, c: (z, y + step, x, c) if c == 0 else (z + step, y, x, c))

    def queries(step):
        return table(lambda z, y, x, c: (z + step, y, x, c) if c == 0 else (z, y + step, x, c))

    def chips(step):
        return table(lambda z, y, x, c: (z, y, x + step, c))

    def cores():
        return table(lambda z, y, x, c: (z, y, x, c + 1))

    return keys, queries, chips, cores


def make_shards(sizes):
    key_move, query_move, chip_move, core_move = ring_moves(sizes)

    def to_key(value, step):
        return lax.ppermute(value, AXES, key_move(step))

    def to_query(value, step):
        return lax.ppermute(value, AXES, query_move(step))

    def shards(query, key_cur, value_cur, d_out, key_hist, value_hist, hist_len):
        same, other, hist0 = pack_call(
            [query, d_out, key_cur, value_cur], key_hist, value_hist, hist_len, sizes
        )
        other = lax.ppermute(other, AXES, core_move())
        hists = [hist0] + [to_key(hist0, -o) for o in OFFSETS[1:]]
        asked, kept = merge_call(same, other)
        kept, hists[1], hists[2] = lax.optimization_barrier((kept, hists[1], hists[2]))

        def exchange(pieces):
            moved = [
                lax.ppermute(p, AXES, chip_move(d)) for p, d in zip(pieces[1:], X_STEPS[1:])
            ]
            return stack_call(pieces[:1] + moved)

        query0 = exchange(asked)
        queries = [query0] + [to_query(query0, -o) for o in OFFSETS[1:]]
        cur0 = exchange(kept)
        curs = [cur0] + [to_key(cur0, -o) for o in OFFSETS[1:]]
        every = (0, 1, 2, 3)
        ends, middle = (0, 3), (1, 2)
        state, kept_a = stats_call(
            curs[:1], hists, [queries[0], queries[3]], ends, saved=SAVED
        )
        state, kept_b = stats_call(curs[:1], hists, queries[1:3], middle, state, saved=SAVED)
        state, kept_c = stats_call(
            curs[1:], [], queries, every, state, fresh=False, saved=(0, 1, 2)
        )
        stats = [state] + [to_query(state, -o) for o in OFFSETS[1:]]
        held = {("cur", 1 + i): [(pair, every)] for i, pair in enumerate(kept_c)}
        for i, a, b in zip(SAVED, kept_a, kept_b):
            name = ("hist", i - 1) if i else ("cur", 0)
            held[name] = [(a, ends), (b, middle)]

        def tiles(*blocks):
            names = [(kind, b) for b in blocks for kind in ("cur", "hist")]
            return {i: held[name] for i, name in enumerate(names) if name in held}

        far, sums = grads_call(curs[3:], hists[3:], queries, stats, tiles(3), whole=(0,))
        far = to_key(far[0], 2)
        (near_m, near_cur, near_hist), sums = grads_call(
            curs[1:3], hists[1:3], queries, stats, tiles(1, 2), sums[0], whole=(0,)
        )
        near_m, near_cur = to_key(near_m, OFFSETS[1]), to_key(near_cur, OFFSETS[2])
        own, sums = grads_call(curs[:1], hists[:1], queries, stats, tiles(0), sums[0], True)
        sums, far = lax.optimization_barrier((sums, far))
        query_parts = [sums[0]] + [to_query(sums[i], OFFSETS[i]) for i in range(1, 4)]

        back = add_call(query_parts, [own[0], far, near_m, near_cur], sizes)
        back, near_hist = lax.optimization_barrier((back, near_hist))
        near_hist = to_key(near_hist, OFFSETS[2])
        back = lax.all_to_all(back, ("x", "c"), 0, 0, tiled=True)
        outs = unpack_call(back, 3)
        grad_k, grad_v = add_hist_call([own[1], near_hist], [far, near_m])
        return outs[0], outs[1], outs[2], grad_k, grad_v

    return shards


def solution(mesh):
    sizes = (4, 4, 4, 2)
    grid = Mesh(mesh.devices.reshape(sizes), AXES)
    token = P(AXES, None)
    hist = P(("z", "y"), ("x", "c"))
    return jax.shard_map(
        make_shards(sizes),
        mesh=grid,
        in_specs=(token, token, token, token, hist, hist, P(("z", "y"))),
        out_specs=(token, token, token, hist, hist),
        check_vma=False,
    )
```

```python
import math

import jax
import jax.numpy as jnp
from jax import lax
from jax.experimental import pallas as pl
from jax.experimental.pallas import tpu as pltpu
from jax.sharding import Mesh
from jax.sharding import PartitionSpec as P

HS = 128
SCALE = 1.0 / math.sqrt(HS)
EXP2_SCALE = SCALE * math.log2(math.e)
LOW = -1e30
VMEM_LIMIT = 12 * 1024 * 1024
PACK_LIMIT = 56 * 1024 * 1024
SAVED = (0, 1, 4)
AXES = ("z", "y", "x", "c")
OFFSETS = (0, -1, 1, 2)
X_STEPS = (0, 1, 3, 2)
F32 = jnp.float32
BF16 = jnp.bfloat16
VMEM = pl.BlockSpec(memory_space=pltpu.VMEM)


def rows_dot(a, b):
    return lax.dot_general(a, b, (((1,), (1,)), ((), ())), preferred_element_type=F32)


def plain_dot(a, b):
    return lax.dot_general(a, b, (((1,), (0,)), ((), ())), preferred_element_type=F32)


def call(kernel, outs, args, flops=0, exps=0, scratch=()):
    size = sum(a.size * a.dtype.itemsize for a in args)
    return pl.pallas_call(
        kernel,
        out_shape=outs,
        in_specs=[VMEM] * len(args),
        out_specs=jax.tree.map(lambda _: VMEM, outs),
        scratch_shapes=list(scratch),
        compiler_params=pltpu.CompilerParams(vmem_limit_bytes=VMEM_LIMIT),
        cost_estimate=pl.CostEstimate(flops=flops // 64, bytes_accessed=size // 64, transcendentals=0),
    )(*args)


def head_lanes(head):
    return pl.ds(pl.multiple_of(head * HS, HS), HS)


def dead_bias(hist, rows, width):
    count = hist[2 * rows : 2 * rows + 16, 0:HS].astype(F32)[0:1]
    slot = lax.broadcasted_iota(jnp.int32, (rows, HS), 0).astype(F32)
    bias = jnp.where(slot < count, 0.0, LOW)
    return jnp.concatenate([bias] * (width // HS), axis=1)


def wide(blocks, which, lanes):
    return jnp.concatenate([block[which, :, lanes] for block in blocks], axis=0)


def stat_step(keys, values, queries, grads, state, bias, keep):
    top, total, dots = state
    scores = rows_dot(keys, queries)
    if bias is not None:
        scores = scores + bias
    new_top = jnp.maximum(top, jnp.max(scores, axis=0, keepdims=True))
    shrink = jnp.exp2((top - new_top) * EXP2_SCALE)
    weights = jnp.exp2((scores - new_top) * EXP2_SCALE)
    grad_scores = rows_dot(values, grads)
    total = total * shrink + jnp.sum(weights, axis=0, keepdims=True)
    dots = dots * shrink + jnp.sum(weights * grad_scores, axis=0, keepdims=True)
    if keep is not None:
        keep(scores, grad_scores)
    return new_top, total, dots


def stats_call(curs, hists, queries, at, state_in=None, fresh=True, saved=()):
    nk, nh, nq = len(curs), len(hists), len(queries)
    tokens, feat = queries[0].shape[1:]
    rows = tokens
    heads = feat // HS
    width = tokens * nq

    def kernel(*refs):
        cur, refs = refs[:nk], refs[nk:]
        hist, refs = refs[:nh], refs[nh:]
        query, refs = refs[:nq], refs[nq:]
        if state_in is not None:
            old, refs = refs[0], refs[1:]
        out, tiles = refs[0], refs[1:]
        if state_in is not None:
            out[...] = old[...]

        def step(head, _):
            lanes = head_lanes(head)
            asked, grads = wide(query, 0, lanes), wide(query, 1, lanes)
            places = [pl.ds(head * 4 + b, 1) for b in at]
            if fresh:
                low, zero = jnp.full((1, width), LOW, F32), jnp.zeros((1, width), F32)
                state = (low, zero, zero)
            else:
                state = tuple(
                    jnp.concatenate([old[i, row, :] for row in places], axis=1) for i in range(3)
                )

            def keep_of(block):
                if block not in saved:
                    return None
                i = saved.index(block)

                def keep(scores, grad_scores):
                    tiles[2 * i][head] = scores
                    tiles[2 * i + 1][head] = grad_scores

                return keep

            for i in range(nk):
                keys, values = cur[i][0, :, lanes], cur[i][1, :, lanes]
                state = stat_step(keys, values, asked, grads, state, None, keep_of(i))
            for i in range(nh):
                keys, values = hist[i][0:rows, lanes], hist[i][rows : 2 * rows, lanes]
                bias = dead_bias(hist[i], rows, width)
                state = stat_step(keys, values, asked, grads, state, bias, keep_of(nk + i))
            for i in range(3):
                for j, row in enumerate(places):
                    out[i, row, :] = state[i][:, j * tokens : (j + 1) * tokens]
            return 0

        lax.fori_loop(0, heads, step, 0)

    args = list(curs) + list(hists) + list(queries) + ([] if state_in is None else [state_in])
    work = (nk + nh) * rows * width
    outs = [jax.ShapeDtypeStruct((3, 16, tokens), F32)]
    outs += [jax.ShapeDtypeStruct((heads, rows, width), F32)] * (2 * len(saved))
    outs = call(kernel, outs, args, flops=2 * 2 * 2 * work * feat, exps=work * heads)
    return outs[0], [tuple(outs[1 + 2 * i : 3 + 2 * i]) for i in range(len(saved))]


def combine_stats(stats, base_ref, delta_ref, heads):
    for head in range(heads):
        for block, offset in enumerate(OFFSETS):
            parts = []
            for ref, step in zip(stats, OFFSETS):
                there = [o % 4 for o in OFFSETS].index((offset - step) % 4)
                row = head * 4 + there
                parts.append([ref[i, row : row + 1, :] for i in range(3)])
            top = jnp.maximum(
                jnp.maximum(parts[0][0], parts[1][0]), jnp.maximum(parts[2][0], parts[3][0])
            )
            total = jnp.zeros_like(top)
            dots = jnp.zeros_like(top)
            for part in parts:
                shrink = jnp.exp2((part[0] - top) * EXP2_SCALE)
                total = total + part[1] * shrink
                dots = dots + part[2] * shrink
            at = slice(block * top.shape[1], (block + 1) * top.shape[1])
            base_ref[head, 0:1, at] = top + jnp.log2(total) * (1.0 / EXP2_SCALE)
            delta_ref[head, 0:1, at] = dots / total


def grads_call(curs, hists, queries, stats, tiles, sums_in=None, last=False, whole=()):
    nk, nq = len(curs), len(queries)
    tokens, feat = queries[0].shape[1:]
    rows = tokens
    heads = feat // HS
    width = nq * tokens
    held = [a for pieces in tiles.values() for pair, _ in pieces for a in pair]

    def kernel(*refs):
        cur, refs = refs[:nk], refs[nk:]
        hist, refs = refs[:nk], refs[nk:]
        query, refs = refs[:nq], refs[nq:]
        stat, refs = refs[:4], refs[4:]
        held_refs, refs = list(refs[: len(held)]), refs[len(held) :]
        found = {
            block: [(held_refs.pop(0), held_refs.pop(0), blocks) for _, blocks in pieces]
            for block, pieces in tiles.items()
        }
        if sums_in is not None:
            old, refs = refs[0], refs[1:]
        key_out, sum_out = refs[:n_out], refs[n_out:-2]
        base, delta = refs[-2:]
        combine_stats(stat, base, delta, heads)

        def saved_tile(block, which, head):
            parts = {}
            for *pair, blocks in found[block]:
                for j, b in enumerate(blocks):
                    parts[b] = pair[which][head, :, j * tokens : (j + 1) * tokens]
            return jnp.concatenate([parts[b] for b in range(nq)], axis=1)

        def part(block, head, keys, values, asked, grads, lift, shift, bias):
            if block in found:
                scores, grad_scores = saved_tile(block, 0, head), saved_tile(block, 1, head)
            else:
                scores, grad_scores = rows_dot(keys, asked), rows_dot(values, grads)
                if bias is not None:
                    scores = scores + bias
            prob = jnp.exp2((scores - lift) * EXP2_SCALE)
            score_grad = (prob * (grad_scores - shift)).astype(BF16)
            grad_v = plain_dot(prob.astype(BF16), grads)
            grad_k = plain_dot(score_grad, asked) * SCALE
            return score_grad, (grad_k, grad_v)

        def step(head, _):
            lanes = head_lanes(head)
            asked, grads = wide(query, 0, lanes), wide(query, 1, lanes)
            lift, shift = base[head, 0:1, :], delta[head, 0:1, :]
            total = None if sums_in is None else old[head]
            for kb in range(nk):
                blocks = [
                    (cur[kb][0, :, lanes], cur[kb][1, :, lanes], None),
                    (
                        hist[kb][0:rows, lanes],
                        hist[kb][rows : 2 * rows, lanes],
                        dead_bias(hist[kb], rows, width),
                    ),
                ]
                all_scores = []
                for i, (keys, values, bias) in enumerate(blocks):
                    score_grad, both = part(
                        2 * kb + i, head, keys, values, asked, grads, lift, shift, bias
                    )
                    all_scores.append(score_grad)
                    for j in range(2):
                        at = firsts[kb]
                        if kb in whole:
                            key_out[at][2 * i + j, :, lanes] = both[j].astype(BF16)
                        else:
                            key_out[at + i][j, :, lanes] = both[j].astype(BF16)
                add = plain_dot(
                    jnp.concatenate([keys for keys, _, _ in blocks], axis=0).T,
                    jnp.concatenate(all_scores, axis=0),
                )
                total = add if total is None else total + add
            if last:
                for b in range(nq):
                    piece = total[:, b * tokens : (b + 1) * tokens] * SCALE
                    sum_out[b][:, lanes] = piece.T.astype(BF16)
            else:
                sum_out[0][head] = total
            return 0

        lax.fori_loop(0, heads, step, 0)

    blocks, firsts = [], []
    for kb in range(nk):
        firsts.append(len(blocks))
        if kb in whole:
            blocks.append(jax.ShapeDtypeStruct((4, rows, feat), BF16))
        else:
            blocks += [jax.ShapeDtypeStruct((2, rows, feat), BF16)] * 2
    n_out = len(blocks)
    if last:
        sums = [jax.ShapeDtypeStruct((tokens, feat), BF16)] * nq
    else:
        sums = [jax.ShapeDtypeStruct((heads, HS, width), F32)]
    args = list(curs) + list(hists) + list(queries) + list(stats) + held
    if sums_in is not None:
        args.append(sums_in)
    work = nk * 2 * rows * width
    outs = call(
        kernel,
        blocks + sums,
        args,
        flops=2 * 5 * 2 * work * feat,
        exps=work * heads,
        scratch=[pltpu.VMEM((heads, 8, width), F32)] * 2,
    )
    return list(outs[:n_out]), list(outs[n_out:])


def pack_call(arrays, key_hist, value_hist, hist_len, sizes):
    rows, columns = arrays[0].shape
    nx, nc = sizes[2:]
    old, feat = key_hist.shape
    n = len(arrays)

    def kernel(*refs):
        ins, (key_in, value_in, count), outs = refs[:n], refs[n : n + 3], refs[n + 3 :]
        same, other, hist, held, sem = outs
        copies = [pltpu.make_async_copy(ref, held.at[i], sem.at[i]) for i, ref in enumerate(ins)]
        copies.append(pltpu.make_async_copy(key_in, hist.at[pl.ds(0, old)], sem.at[n]))
        copies.append(pltpu.make_async_copy(value_in, hist.at[pl.ds(old, old)], sem.at[n + 1]))
        for copy in copies:
            copy.start()
        filled = jnp.full((16, feat), count[0], jnp.int32).astype(F32)
        hist[2 * old :, :] = filled.astype(BF16)
        x, core = lax.axis_index("x"), lax.axis_index("c")
        for i in range(n):
            copies[i].wait()
            for j, step in enumerate(X_STEPS):
                for k, out in enumerate((same, other)):
                    part = lax.rem(x + step, nx) * nc + lax.rem(core + k, nc)
                    at = pl.ds(pl.multiple_of(part * feat, feat), feat)
                    out[i // 2, j, i % 2] = held[i, :, at]
        copies[n].wait()
        copies[n + 1].wait()

    shape = jax.ShapeDtypeStruct((n // 2, nx, 2, rows, feat), BF16)
    return pl.pallas_call(
        kernel,
        out_shape=[shape, shape, jax.ShapeDtypeStruct((2 * old + 16, feat), BF16)],
        in_specs=[pl.BlockSpec(memory_space=pl.ANY)] * (n + 2)
        + [pl.BlockSpec(memory_space=pltpu.SMEM)],
        out_specs=[VMEM] * 3,
        scratch_shapes=[
            pltpu.VMEM((n, rows, columns), BF16),
            pltpu.SemaphoreType.DMA((n + 2,)),
        ],
        compiler_params=pltpu.CompilerParams(vmem_limit_bytes=PACK_LIMIT),
    )(*arrays, key_hist, value_hist, hist_len)


def merge_call(same, other):
    pairs, nx, two, rows, feat = same.shape

    def kernel(a, b, *outs):
        for i in range(pairs):
            for j in range(nx):
                outs[i * nx + j][:, 0:rows, :] = a[i, j]
                outs[i * nx + j][:, rows : 2 * rows, :] = b[i, j]

    shape = jax.ShapeDtypeStruct((two, 2 * rows, feat), BF16)
    outs = call(kernel, [shape] * (pairs * nx), [same, other])
    return [list(outs[i * nx : (i + 1) * nx]) for i in range(pairs)]


def stack_call(blocks):
    two, rows, feat = blocks[0].shape

    def kernel(*refs):
        for j, ref in enumerate(refs[:-1]):
            refs[-1][:, j * rows : (j + 1) * rows, :] = ref[...]

    shape = jax.ShapeDtypeStruct((two, len(blocks) * rows, feat), BF16)
    return call(kernel, shape, blocks)


def finish_call(pieces, other, sizes, parts, whole):
    nx, count, rows, feat = other.shape
    nc = sizes[3]
    old = whole[0].shape[1]
    n = len(parts)

    def kernel(*refs):
        mine, rest, refs = refs[:nx], refs[nx], refs[nx + 1 :]
        terms, outs, sums = refs[: -count - 2], refs[-count - 2 : -2], refs[-2:]
        x, core = lax.axis_index("x"), lax.axis_index("c")
        for i, out in enumerate(sums):
            total = sum(term[i].astype(F32) for term in terms[:n])
            total = total + sum(term[2 + i].astype(F32) for term in terms[n:])
            out[...] = total.astype(BF16)
        for j, step in enumerate(X_STEPS):
            for k in range(nc):
                part = lax.rem(x + step, nx) * nc + lax.rem(core + k, nc)
                at = pl.ds(pl.multiple_of(part * feat, feat), feat)
                for i, out in enumerate(outs):
                    out[:, at] = mine[j][i, 0:rows] if k == 0 else rest[j, i]

    shapes = [jax.ShapeDtypeStruct((rows, nx * nc * feat), BF16)] * count
    shapes += [jax.ShapeDtypeStruct((old, feat), BF16)] * 2
    return call(kernel, shapes, [*pieces, other, *parts, *whole])


def add_call(query_parts, cur_parts, pieces):
    tokens, feat = query_parts[0].shape
    rows = tokens // pieces
    nq = len(query_parts)

    def kernel(*refs):
        ins, outs = refs[:-pieces], refs[-pieces:]
        sums = [
            sum(ref[...].astype(F32) for ref in ins[:nq]),
            sum(ref[0].astype(F32) for ref in ins[nq:]),
            sum(ref[1].astype(F32) for ref in ins[nq:]),
        ]
        for i, total in enumerate(sums):
            low = total.astype(BF16)
            for j, out in enumerate(outs):
                out[i] = low[j * rows : (j + 1) * rows]

    shape = jax.ShapeDtypeStruct((3, rows, feat), BF16)
    return list(call(kernel, [shape] * pieces, list(query_parts) + list(cur_parts)))


def other_call(pieces):
    count, rows, feat = pieces[0].shape
    rows //= 2

    def kernel(*refs):
        for j, ref in enumerate(refs[:-1]):
            refs[-1][j] = ref[:, rows:, :]

    shape = jax.ShapeDtypeStruct((len(pieces), count, rows, feat), BF16)
    return call(kernel, shape, list(pieces))


def ring_moves(sizes):
    nz, ny, nx, nc = sizes

    def table(target):
        pairs = []
        for z in range(nz):
            for y in range(ny):
                for x in range(nx):
                    for c in range(nc):
                        tz, ty, tx, tc = target(z, y, x, c)
                        src = ((z * ny + y) * nx + x) * nc + c
                        dst = ((tz % nz) * ny + ty % ny) * nx + tx % nx
                        pairs.append((src, dst * nc + tc % nc))
        return pairs

    def keys(step):
        return table(lambda z, y, x, c: (z, y + step, x, c) if c == 0 else (z + step, y, x, c))

    def queries(step):
        return table(lambda z, y, x, c: (z + step, y, x, c) if c == 0 else (z, y + step, x, c))

    def chips(step):
        return table(lambda z, y, x, c: (z, y, x + step, c))

    def cores():
        return table(lambda z, y, x, c: (z, y, x, c + 1))

    return keys, queries, chips, cores


def make_shards(sizes):
    key_move, query_move, chip_move, core_move = ring_moves(sizes)

    def to_key(value, step):
        return lax.ppermute(value, AXES, key_move(step))

    def to_query(value, step):
        return lax.ppermute(value, AXES, query_move(step))

    def shards(query, key_cur, value_cur, d_out, key_hist, value_hist, hist_len):
        same, other, hist0 = pack_call(
            [query, d_out, key_cur, value_cur], key_hist, value_hist, hist_len, sizes
        )
        other = lax.ppermute(other, AXES, core_move())
        hists = [hist0] + [to_key(hist0, -o) for o in OFFSETS[1:]]
        asked, kept = merge_call(same, other)
        kept, hists[1], hists[2] = lax.optimization_barrier((kept, hists[1], hists[2]))

        def exchange(pieces):
            moved = [
                lax.ppermute(p, AXES, chip_move(d)) for p, d in zip(pieces[1:], X_STEPS[1:])
            ]
            return stack_call(pieces[:1] + moved)

        query0 = exchange(asked)
        queries = [query0] + [to_query(query0, -o) for o in OFFSETS[1:]]
        cur0 = exchange(kept)
        curs = [cur0] + [to_key(cur0, -o) for o in OFFSETS[1:]]
        every = (0, 1, 2, 3)
        ends, middle = (0, 3), (1, 2)
        state, kept_a = stats_call(
            curs[:1], hists, [queries[0], queries[3]], ends, saved=SAVED
        )
        state, kept_b = stats_call(curs[:1], hists, queries[1:3], middle, state, saved=SAVED)
        state, kept_c = stats_call(
            curs[1:], [], queries, every, state, fresh=False, saved=(0, 1, 2)
        )
        stats = [state] + [to_query(state, -o) for o in OFFSETS[1:]]
        held = {("cur", 1 + i): [(pair, every)] for i, pair in enumerate(kept_c)}
        for i, a, b in zip(SAVED, kept_a, kept_b):
            name = ("hist", i - 1) if i else ("cur", 0)
            held[name] = [(a, ends), (b, middle)]

        def tiles(*blocks):
            names = [(kind, b) for b in blocks for kind in ("cur", "hist")]
            return {i: held[name] for i, name in enumerate(names) if name in held}

        far, sums = grads_call(curs[3:], hists[3:], queries, stats, tiles(3), whole=(0,))
        far = to_key(far[0], 2)
        (near_m, near_cur, near_hist), sums = grads_call(
            curs[1:3], hists[1:3], queries, stats, tiles(1, 2), sums[0], whole=(0,)
        )
        near_m, near_cur = to_key(near_m, OFFSETS[1]), to_key(near_cur, OFFSETS[2])
        own, sums = grads_call(curs[:1], hists[:1], queries, stats, tiles(0), sums[0], True)
        sums, far = lax.optimization_barrier((sums, far))
        query_parts = [sums[0]] + [to_query(sums[i], OFFSETS[i]) for i in range(1, 4)]

        back = add_call(query_parts, [own[0], far, near_m, near_cur], sizes[2])
        back, near_hist = lax.optimization_barrier((back, near_hist))
        near_hist = to_key(near_hist, OFFSETS[2])
        moved = [lax.ppermute(p, AXES, chip_move(-d)) for p, d in zip(back[1:], X_STEPS[1:])]
        back = back[:1] + moved
        other = lax.ppermute(other_call(back), AXES, core_move())
        return tuple(finish_call(back, other, sizes, [own[1], near_hist], [far, near_m]))

    return shards


def solution(mesh):
    sizes = (4, 4, 4, 2)
    grid = Mesh(mesh.devices.reshape(sizes), AXES)
    token = P(AXES, None)
    hist = P(("z", "y"), ("x", "c"))
    return jax.shard_map(
        make_shards(sizes),
        mesh=grid,
        in_specs=(token, token, token, token, hist, hist, P(("z", "y"))),
        out_specs=(token, token, token, hist, hist),
        check_vma=False,
    )
```

```python
import math

import jax
import jax.numpy as jnp
from jax import lax
from jax.experimental import pallas as pl
from jax.experimental.pallas import tpu as pltpu
from jax.sharding import Mesh
from jax.sharding import PartitionSpec as P

HS = 128
SCALE = 1.0 / math.sqrt(HS)
EXP2_SCALE = SCALE * math.log2(math.e)
LOW = -1e30
VMEM_LIMIT = 12 * 1024 * 1024
PACK_LIMIT = 56 * 1024 * 1024
SAVED = (0, 1, 4)
AXES = ("z", "y", "x", "c")
OFFSETS = (0, -1, 1, 2)
X_STEPS = (0, 1, 3, 2)
F32 = jnp.float32
BF16 = jnp.bfloat16
VMEM = pl.BlockSpec(memory_space=pltpu.VMEM)


def rows_dot(a, b):
    return lax.dot_general(a, b, (((1,), (1,)), ((), ())), preferred_element_type=F32)


def plain_dot(a, b):
    return lax.dot_general(a, b, (((1,), (0,)), ((), ())), preferred_element_type=F32)


def call(kernel, outs, args, flops=0, exps=0, scratch=()):
    size = sum(a.size * a.dtype.itemsize for a in args)
    return pl.pallas_call(
        kernel,
        out_shape=outs,
        in_specs=[VMEM] * len(args),
        out_specs=jax.tree.map(lambda _: VMEM, outs),
        scratch_shapes=list(scratch),
        compiler_params=pltpu.CompilerParams(vmem_limit_bytes=VMEM_LIMIT),
        cost_estimate=pl.CostEstimate(flops=flops // 64, bytes_accessed=size // 64, transcendentals=0),
    )(*args)


def head_lanes(head):
    return pl.ds(pl.multiple_of(head * HS, HS), HS)


def dead_bias(hist, rows, width):
    count = hist[2 * rows : 2 * rows + 16, 0:HS].astype(F32)[0:1]
    slot = lax.broadcasted_iota(jnp.int32, (rows, HS), 0).astype(F32)
    bias = jnp.where(slot < count, 0.0, LOW)
    return jnp.concatenate([bias] * (width // HS), axis=1)


def wide(blocks, which, lanes):
    return jnp.concatenate([block[which, :, lanes] for block in blocks], axis=0)


def stat_step(keys, values, queries, grads, state, bias, keep):
    top, total, dots = state
    scores = rows_dot(keys, queries)
    if bias is not None:
        scores = scores + bias
    new_top = jnp.maximum(top, jnp.max(scores, axis=0, keepdims=True))
    shrink = jnp.exp2((top - new_top) * EXP2_SCALE)
    weights = jnp.exp2((scores - new_top) * EXP2_SCALE)
    grad_scores = rows_dot(values, grads)
    total = total * shrink + jnp.sum(weights, axis=0, keepdims=True)
    dots = dots * shrink + jnp.sum(weights * grad_scores, axis=0, keepdims=True)
    if keep is not None:
        keep(scores, grad_scores)
    return new_top, total, dots


def stats_call(curs, hists, queries, at, state_in=None, fresh=True, saved=()):
    nk, nh, nq = len(curs), len(hists), len(queries)
    tokens, feat = queries[0].shape[1:]
    rows = tokens
    heads = feat // HS
    width = tokens * nq

    def kernel(*refs):
        cur, refs = refs[:nk], refs[nk:]
        hist, refs = refs[:nh], refs[nh:]
        query, refs = refs[:nq], refs[nq:]
        if state_in is not None:
            old, refs = refs[0], refs[1:]
        out, tiles = refs[0], refs[1:]
        if state_in is not None:
            out[...] = old[...]

        def step(head, _):
            lanes = head_lanes(head)
            asked, grads = wide(query, 0, lanes), wide(query, 1, lanes)
            places = [pl.ds(head * 4 + b, 1) for b in at]
            if fresh:
                low, zero = jnp.full((1, width), LOW, F32), jnp.zeros((1, width), F32)
                state = (low, zero, zero)
            else:
                state = tuple(
                    jnp.concatenate([old[i, row, :] for row in places], axis=1) for i in range(3)
                )

            def keep_of(block):
                if block not in saved:
                    return None
                i = saved.index(block)

                def keep(scores, grad_scores):
                    tiles[2 * i][head] = scores
                    tiles[2 * i + 1][head] = grad_scores

                return keep

            for i in range(nk):
                keys, values = cur[i][0, :, lanes], cur[i][1, :, lanes]
                state = stat_step(keys, values, asked, grads, state, None, keep_of(i))
            for i in range(nh):
                keys, values = hist[i][0:rows, lanes], hist[i][rows : 2 * rows, lanes]
                bias = dead_bias(hist[i], rows, width)
                state = stat_step(keys, values, asked, grads, state, bias, keep_of(nk + i))
            for i in range(3):
                for j, row in enumerate(places):
                    out[i, row, :] = state[i][:, j * tokens : (j + 1) * tokens]
            return 0

        lax.fori_loop(0, heads, step, 0)

    args = list(curs) + list(hists) + list(queries) + ([] if state_in is None else [state_in])
    work = (nk + nh) * rows * width
    outs = [jax.ShapeDtypeStruct((3, 16, tokens), F32)]
    outs += [jax.ShapeDtypeStruct((heads, rows, width), F32)] * (2 * len(saved))
    outs = call(kernel, outs, args, flops=2 * 2 * 2 * work * feat, exps=work * heads)
    return outs[0], [tuple(outs[1 + 2 * i : 3 + 2 * i]) for i in range(len(saved))]


def combine_stats(stats, base_ref, delta_ref, heads):
    for head in range(heads):
        for block, offset in enumerate(OFFSETS):
            parts = []
            for ref, step in zip(stats, OFFSETS):
                there = [o % 4 for o in OFFSETS].index((offset - step) % 4)
                row = head * 4 + there
                parts.append([ref[i, row : row + 1, :] for i in range(3)])
            top = jnp.maximum(
                jnp.maximum(parts[0][0], parts[1][0]), jnp.maximum(parts[2][0], parts[3][0])
            )
            total = jnp.zeros_like(top)
            dots = jnp.zeros_like(top)
            for part in parts:
                shrink = jnp.exp2((part[0] - top) * EXP2_SCALE)
                total = total + part[1] * shrink
                dots = dots + part[2] * shrink
            at = slice(block * top.shape[1], (block + 1) * top.shape[1])
            base_ref[head, 0:1, at] = top + jnp.log2(total) * (1.0 / EXP2_SCALE)
            delta_ref[head, 0:1, at] = dots / total


def grads_call(curs, hists, queries, stats, tiles, sums_in=None, last=False, whole=()):
    nk, nq = len(curs), len(queries)
    tokens, feat = queries[0].shape[1:]
    rows = tokens
    heads = feat // HS
    width = nq * tokens
    held = [a for pieces in tiles.values() for pair, _ in pieces for a in pair]

    def kernel(*refs):
        cur, refs = refs[:nk], refs[nk:]
        hist, refs = refs[:nk], refs[nk:]
        query, refs = refs[:nq], refs[nq:]
        stat, refs = refs[:4], refs[4:]
        held_refs, refs = list(refs[: len(held)]), refs[len(held) :]
        found = {
            block: [(held_refs.pop(0), held_refs.pop(0), blocks) for _, blocks in pieces]
            for block, pieces in tiles.items()
        }
        if sums_in is not None:
            old, refs = refs[0], refs[1:]
        key_out, sum_out = refs[:n_out], refs[n_out:-2]
        base, delta = refs[-2:]
        combine_stats(stat, base, delta, heads)

        def saved_tile(block, which, head):
            parts = {}
            for *pair, blocks in found[block]:
                for j, b in enumerate(blocks):
                    parts[b] = pair[which][head, :, j * tokens : (j + 1) * tokens]
            return jnp.concatenate([parts[b] for b in range(nq)], axis=1)

        def part(block, head, keys, values, asked, grads, lift, shift, bias):
            if block in found:
                scores, grad_scores = saved_tile(block, 0, head), saved_tile(block, 1, head)
            else:
                scores, grad_scores = rows_dot(keys, asked), rows_dot(values, grads)
                if bias is not None:
                    scores = scores + bias
            prob = jnp.exp2((scores - lift) * EXP2_SCALE)
            score_grad = (prob * (grad_scores - shift)).astype(BF16)
            grad_v = plain_dot(prob.astype(BF16), grads)
            grad_k = plain_dot(score_grad, asked) * SCALE
            return score_grad, (grad_k, grad_v)

        def step(head, _):
            lanes = head_lanes(head)
            asked, grads = wide(query, 0, lanes), wide(query, 1, lanes)
            lift, shift = base[head, 0:1, :], delta[head, 0:1, :]
            total = None if sums_in is None else old[head]
            for kb in range(nk):
                blocks = [
                    (cur[kb][0, :, lanes], cur[kb][1, :, lanes], None),
                    (
                        hist[kb][0:rows, lanes],
                        hist[kb][rows : 2 * rows, lanes],
                        dead_bias(hist[kb], rows, width),
                    ),
                ]
                all_scores = []
                for i, (keys, values, bias) in enumerate(blocks):
                    score_grad, both = part(
                        2 * kb + i, head, keys, values, asked, grads, lift, shift, bias
                    )
                    all_scores.append(score_grad)
                    for j in range(2):
                        at = firsts[kb]
                        if kb in whole:
                            key_out[at][2 * i + j, :, lanes] = both[j].astype(BF16)
                        else:
                            key_out[at + i][j, :, lanes] = both[j].astype(BF16)
                add = plain_dot(
                    jnp.concatenate([keys for keys, _, _ in blocks], axis=0).T,
                    jnp.concatenate(all_scores, axis=0),
                )
                total = add if total is None else total + add
            if last:
                for b in range(nq):
                    piece = total[:, b * tokens : (b + 1) * tokens] * SCALE
                    sum_out[b][:, lanes] = piece.T.astype(BF16)
            else:
                sum_out[0][head] = total
            return 0

        lax.fori_loop(0, heads, step, 0)

    blocks, firsts = [], []
    for kb in range(nk):
        firsts.append(len(blocks))
        if kb in whole:
            blocks.append(jax.ShapeDtypeStruct((4, rows, feat), BF16))
        else:
            blocks += [jax.ShapeDtypeStruct((2, rows, feat), BF16)] * 2
    n_out = len(blocks)
    if last:
        sums = [jax.ShapeDtypeStruct((tokens, feat), BF16)] * nq
    else:
        sums = [jax.ShapeDtypeStruct((heads, HS, width), F32)]
    args = list(curs) + list(hists) + list(queries) + list(stats) + held
    if sums_in is not None:
        args.append(sums_in)
    work = nk * 2 * rows * width
    outs = call(
        kernel,
        blocks + sums,
        args,
        flops=2 * 5 * 2 * work * feat,
        exps=work * heads,
        scratch=[pltpu.VMEM((heads, 8, width), F32)] * 2,
    )
    return list(outs[:n_out]), list(outs[n_out:])


def pack_call(arrays, key_hist, value_hist, hist_len, sizes):
    rows, columns = arrays[0].shape
    nx, nc = sizes[2:]
    old, feat = key_hist.shape
    n = len(arrays)

    def kernel(*refs):
        ins, (key_in, value_in, count), outs = refs[:n], refs[n : n + 3], refs[n + 3 :]
        same, other, hist, held, sem = outs
        copies = [pltpu.make_async_copy(ref, held.at[i], sem.at[i]) for i, ref in enumerate(ins)]
        copies.append(pltpu.make_async_copy(key_in, hist.at[pl.ds(0, old)], sem.at[n]))
        copies.append(pltpu.make_async_copy(value_in, hist.at[pl.ds(old, old)], sem.at[n + 1]))
        for copy in copies:
            copy.start()
        filled = jnp.full((16, feat), count[0], jnp.int32).astype(F32)
        hist[2 * old :, :] = filled.astype(BF16)
        x, core = lax.axis_index("x"), lax.axis_index("c")
        for i in range(n):
            copies[i].wait()
            for j, step in enumerate(X_STEPS):
                for k, out in enumerate((same, other)):
                    part = lax.rem(x + step, nx) * nc + lax.rem(core + k, nc)
                    at = pl.ds(pl.multiple_of(part * feat, feat), feat)
                    out[i // 2, j, i % 2] = held[i, :, at]
        copies[n].wait()
        copies[n + 1].wait()

    shape = jax.ShapeDtypeStruct((n // 2, nx, 2, rows, feat), BF16)
    return pl.pallas_call(
        kernel,
        out_shape=[shape, shape, jax.ShapeDtypeStruct((2 * old + 16, feat), BF16)],
        in_specs=[pl.BlockSpec(memory_space=pl.ANY)] * (n + 2)
        + [pl.BlockSpec(memory_space=pltpu.SMEM)],
        out_specs=[VMEM] * 3,
        scratch_shapes=[
            pltpu.VMEM((n, rows, columns), BF16),
            pltpu.SemaphoreType.DMA((n + 2,)),
        ],
        compiler_params=pltpu.CompilerParams(vmem_limit_bytes=PACK_LIMIT),
    )(*arrays, key_hist, value_hist, hist_len)


def merge_call(same, other):
    pairs, nx, two, rows, feat = same.shape

    def kernel(a, b, *outs):
        for i in range(pairs):
            for j in range(nx):
                outs[i * nx + j][:, 0:rows, :] = a[i, j]
                outs[i * nx + j][:, rows : 2 * rows, :] = b[i, j]

    shape = jax.ShapeDtypeStruct((two, 2 * rows, feat), BF16)
    outs = call(kernel, [shape] * (pairs * nx), [same, other])
    return [list(outs[i * nx : (i + 1) * nx]) for i in range(pairs)]


def stack_call(blocks):
    two, rows, feat = blocks[0].shape

    def kernel(*refs):
        for j, ref in enumerate(refs[:-1]):
            refs[-1][:, j * rows : (j + 1) * rows, :] = ref[...]

    shape = jax.ShapeDtypeStruct((two, len(blocks) * rows, feat), BF16)
    return call(kernel, shape, blocks)


def finish_call(pieces, other, sizes, parts, whole):
    nx, count, rows, feat = other.shape
    nc = sizes[3]
    old = whole[0].shape[1]
    n = len(parts)

    def kernel(*refs):
        mine, rest, refs = refs[:nx], refs[nx], refs[nx + 1 :]
        terms, outs, sums = refs[: -count - 2], refs[-count - 2 : -2], refs[-2:]
        x, core = lax.axis_index("x"), lax.axis_index("c")
        for i, out in enumerate(sums):
            total = sum(term[i].astype(F32) for term in terms[:n])
            total = total + sum(term[2 + i].astype(F32) for term in terms[n:])
            out[...] = total.astype(BF16)
        for j, step in enumerate(X_STEPS):
            for k in range(nc):
                part = lax.rem(x + step, nx) * nc + lax.rem(core + k, nc)
                at = pl.ds(pl.multiple_of(part * feat, feat), feat)
                for i, out in enumerate(outs):
                    out[:, at] = mine[j][i, 0:rows] if k == 0 else rest[j, i]

    shapes = [jax.ShapeDtypeStruct((rows, nx * nc * feat), BF16)] * count
    shapes += [jax.ShapeDtypeStruct((old, feat), BF16)] * 2
    return call(kernel, shapes, [*pieces, other, *parts, *whole])


def add_call(query_parts, cur_parts, pieces):
    tokens, feat = query_parts[0].shape
    rows = tokens // pieces
    nq = len(query_parts)

    def kernel(*refs):
        ins, outs = refs[:-pieces], refs[-pieces:]
        sums = [
            sum(ref[...].astype(F32) for ref in ins[:nq]),
            sum(ref[0].astype(F32) for ref in ins[nq:]),
            sum(ref[1].astype(F32) for ref in ins[nq:]),
        ]
        for i, total in enumerate(sums):
            low = total.astype(BF16)
            for j, out in enumerate(outs):
                out[i] = low[j * rows : (j + 1) * rows]

    shape = jax.ShapeDtypeStruct((3, rows, feat), BF16)
    return list(call(kernel, [shape] * pieces, list(query_parts) + list(cur_parts)))


def other_call(pieces):
    count, rows, feat = pieces[0].shape
    rows //= 2

    def kernel(*refs):
        for j, ref in enumerate(refs[:-1]):
            refs[-1][j] = ref[:, rows:, :]

    shape = jax.ShapeDtypeStruct((len(pieces), count, rows, feat), BF16)
    return call(kernel, shape, list(pieces))


def ring_moves(sizes):
    nz, ny, nx, nc = sizes

    def table(target):
        pairs = []
        for z in range(nz):
            for y in range(ny):
                for x in range(nx):
                    for c in range(nc):
                        tz, ty, tx, tc = target(z, y, x, c)
                        src = ((z * ny + y) * nx + x) * nc + c
                        dst = ((tz % nz) * ny + ty % ny) * nx + tx % nx
                        pairs.append((src, dst * nc + tc % nc))
        return pairs

    def keys(step):
        return table(lambda z, y, x, c: (z, y + step, x, c) if c == 0 else (z + step, y, x, c))

    def queries(step):
        return table(lambda z, y, x, c: (z + step, y, x, c) if c == 0 else (z, y + step, x, c))

    def chips(step):
        return table(lambda z, y, x, c: (z, y, x + step, c))

    def cores():
        return table(lambda z, y, x, c: (z, y, x, c + 1))

    return keys, queries, chips, cores


def make_shards(sizes):
    key_move, query_move, chip_move, core_move = ring_moves(sizes)

    def to_key(value, step):
        return lax.ppermute(value, AXES, key_move(step))

    def to_query(value, step):
        return lax.ppermute(value, AXES, query_move(step))

    def shards(query, key_cur, value_cur, d_out, key_hist, value_hist, hist_len):
        same, other, hist0 = pack_call(
            [query, d_out, key_cur, value_cur], key_hist, value_hist, hist_len, sizes
        )
        other = lax.ppermute(other, AXES, core_move())
        hists = [hist0] + [to_key(hist0, -o) for o in OFFSETS[1:]]
        asked, kept = merge_call(same, other)
        kept, hists[1], hists[2] = lax.optimization_barrier((kept, hists[1], hists[2]))

        def exchange(pieces):
            moved = [
                lax.ppermute(p, AXES, chip_move(d)) for p, d in zip(pieces[1:], X_STEPS[1:])
            ]
            return stack_call(pieces[:1] + moved)

        query0 = exchange(asked)
        queries = [query0] + [to_query(query0, -o) for o in OFFSETS[1:]]
        cur0 = exchange(kept)
        curs = [cur0] + [to_key(cur0, -o) for o in OFFSETS[1:]]
        every = (0, 1, 2, 3)
        ends, middle = (0, 3), (1, 2)
        state, kept_a = stats_call(
            curs[:1], hists, [queries[0], queries[3]], ends, saved=SAVED
        )
        state, kept_b = stats_call(curs[:1], hists, queries[1:3], middle, state, saved=SAVED)
        state, kept_c = stats_call(
            curs[1:], [], queries, every, state, fresh=False, saved=(0, 1, 2)
        )
        stats = [state] + [to_query(state, -o) for o in OFFSETS[1:]]
        held = {("cur", 1 + i): [(pair, every)] for i, pair in enumerate(kept_c)}
        for i, a, b in zip(SAVED, kept_a, kept_b):
            name = ("hist", i - 1) if i else ("cur", 0)
            held[name] = [(a, ends), (b, middle)]

        def tiles(*blocks):
            names = [(kind, b) for b in blocks for kind in ("cur", "hist")]
            return {i: held[name] for i, name in enumerate(names) if name in held}

        far, sums = grads_call(curs[3:], hists[3:], queries, stats, tiles(3), whole=(0,))
        far = to_key(far[0], 2)
        (near_cur, near_hist, near_p), sums = grads_call(
            curs[1:3], hists[1:3], queries, stats, tiles(1, 2), sums[0], whole=(1,)
        )
        near_cur, near_p = to_key(near_cur, OFFSETS[1]), to_key(near_p, OFFSETS[2])
        own, sums = grads_call(curs[:1], hists[:1], queries, stats, tiles(0), sums[0], True)
        sums, far = lax.optimization_barrier((sums, far))
        query_parts = [sums[0]] + [to_query(sums[i], OFFSETS[i]) for i in range(1, 4)]

        back = add_call(query_parts, [own[0], far, near_cur, near_p], sizes[2])
        back, near_hist = lax.optimization_barrier((back, near_hist))
        near_hist = to_key(near_hist, OFFSETS[1])
        moved = [lax.ppermute(p, AXES, chip_move(-d)) for p, d in zip(back[1:], X_STEPS[1:])]
        back = back[:1] + moved
        other = lax.ppermute(other_call(back), AXES, core_move())
        return tuple(finish_call(back, other, sizes, [own[1], near_hist], [far, near_p]))

    return shards


def solution(mesh):
    sizes = (4, 4, 4, 2)
    grid = Mesh(mesh.devices.reshape(sizes), AXES)
    token = P(AXES, None)
    hist = P(("z", "y"), ("x", "c"))
    return jax.shard_map(
        make_shards(sizes),
        mesh=grid,
        in_specs=(token, token, token, token, hist, hist, P(("z", "y"))),
        out_specs=(token, token, token, hist, hist),
        check_vma=False,
    )
```

```python
import math

import jax
import jax.numpy as jnp
from jax import lax
from jax.experimental import pallas as pl
from jax.experimental.pallas import tpu as pltpu
from jax.sharding import Mesh
from jax.sharding import PartitionSpec as P

HS = 128
SCALE = 1.0 / math.sqrt(HS)
EXP2_SCALE = SCALE * math.log2(math.e)
LOW = -1e30
VMEM_LIMIT = 6 * 1024 * 1024
PACK_LIMIT = 56 * 1024 * 1024
SAVED = (0, 1, 2, 4)
AXES = ("z", "y", "x", "c")
OFFSETS = (0, -1, 1, 2)
X_STEPS = (0, 1, 3, 2)
F32 = jnp.float32
BF16 = jnp.bfloat16
VMEM = pl.BlockSpec(memory_space=pltpu.VMEM)


def rows_dot(a, b):
    return lax.dot_general(a, b, (((1,), (1,)), ((), ())), preferred_element_type=F32)


def plain_dot(a, b):
    return lax.dot_general(a, b, (((1,), (0,)), ((), ())), preferred_element_type=F32)


def call(kernel, outs, args, flops=0, exps=0, scratch=()):
    size = sum(a.size * a.dtype.itemsize for a in args)
    return pl.pallas_call(
        kernel,
        out_shape=outs,
        in_specs=[VMEM] * len(args),
        out_specs=jax.tree.map(lambda _: VMEM, outs),
        scratch_shapes=list(scratch),
        compiler_params=pltpu.CompilerParams(vmem_limit_bytes=VMEM_LIMIT),
        cost_estimate=pl.CostEstimate(flops=flops // 64, bytes_accessed=size // 64, transcendentals=0),
    )(*args)


def head_lanes(head):
    return pl.ds(pl.multiple_of(head * HS, HS), HS)


def dead_bias(hist, rows, width):
    count = hist[2 * rows : 2 * rows + 16, 0:HS].astype(F32)[0:1]
    slot = lax.broadcasted_iota(jnp.int32, (rows, HS), 0).astype(F32)
    bias = jnp.where(slot < count, 0.0, LOW)
    return jnp.concatenate([bias] * (width // HS), axis=1)


def wide(blocks, which, lanes):
    return jnp.concatenate([block[which, :, lanes] for block in blocks], axis=0)


def stat_step(keys, values, queries, grads, state, bias, keep):
    top, total, dots = state
    scores = rows_dot(keys, queries)
    if bias is not None:
        scores = scores + bias
    new_top = jnp.maximum(top, jnp.max(scores, axis=0, keepdims=True))
    shrink = jnp.exp2((top - new_top) * EXP2_SCALE)
    weights = jnp.exp2((scores - new_top) * EXP2_SCALE)
    grad_scores = rows_dot(values, grads)
    total = total * shrink + jnp.sum(weights, axis=0, keepdims=True)
    dots = dots * shrink + jnp.sum(weights * grad_scores, axis=0, keepdims=True)
    if keep is not None:
        keep(scores, grad_scores)
    return new_top, total, dots


def stats_call(curs, hists, queries, at, state_in=None, fresh=True, saved=()):
    nk, nh, nq = len(curs), len(hists), len(queries)
    tokens, feat = queries[0].shape[1:]
    rows = tokens
    heads = feat // HS
    width = tokens * nq

    def kernel(*refs):
        cur, refs = refs[:nk], refs[nk:]
        hist, refs = refs[:nh], refs[nh:]
        query, refs = refs[:nq], refs[nq:]
        if state_in is not None:
            old, refs = refs[0], refs[1:]
        out, tiles = refs[0], refs[1:]
        if state_in is not None:
            out[...] = old[...]

        def step(head, _):
            lanes = head_lanes(head)
            asked, grads = wide(query, 0, lanes), wide(query, 1, lanes)
            places = [pl.ds(head * 4 + b, 1) for b in at]
            if fresh:
                low, zero = jnp.full((1, width), LOW, F32), jnp.zeros((1, width), F32)
                state = (low, zero, zero)
            else:
                state = tuple(
                    jnp.concatenate([old[i, row, :] for row in places], axis=1) for i in range(3)
                )

            def keep_of(block):
                if block not in saved:
                    return None
                i = saved.index(block)

                def keep(scores, grad_scores):
                    tiles[2 * i][head] = scores
                    tiles[2 * i + 1][head] = grad_scores

                return keep

            for i in range(nk):
                keys, values = cur[i][0, :, lanes], cur[i][1, :, lanes]
                state = stat_step(keys, values, asked, grads, state, None, keep_of(i))
            for i in range(nh):
                keys, values = hist[i][0:rows, lanes], hist[i][rows : 2 * rows, lanes]
                bias = dead_bias(hist[i], rows, width)
                state = stat_step(keys, values, asked, grads, state, bias, keep_of(nk + i))
            for i in range(3):
                for j, row in enumerate(places):
                    out[i, row, :] = state[i][:, j * tokens : (j + 1) * tokens]
            return 0

        lax.fori_loop(0, heads, step, 0)

    args = list(curs) + list(hists) + list(queries) + ([] if state_in is None else [state_in])
    work = (nk + nh) * rows * width
    outs = [jax.ShapeDtypeStruct((3, 16, tokens), F32)]
    outs += [jax.ShapeDtypeStruct((heads, rows, width), F32)] * (2 * len(saved))
    outs = call(kernel, outs, args, flops=2 * 2 * 2 * work * feat, exps=work * heads)
    return outs[0], [tuple(outs[1 + 2 * i : 3 + 2 * i]) for i in range(len(saved))]


def combine_stats(stats, base_ref, delta_ref, heads):
    for head in range(heads):
        for block, offset in enumerate(OFFSETS):
            parts = []
            for ref, step in zip(stats, OFFSETS):
                there = [o % 4 for o in OFFSETS].index((offset - step) % 4)
                row = head * 4 + there
                parts.append([ref[i, row : row + 1, :] for i in range(3)])
            top = jnp.maximum(
                jnp.maximum(parts[0][0], parts[1][0]), jnp.maximum(parts[2][0], parts[3][0])
            )
            total = jnp.zeros_like(top)
            dots = jnp.zeros_like(top)
            for part in parts:
                shrink = jnp.exp2((part[0] - top) * EXP2_SCALE)
                total = total + part[1] * shrink
                dots = dots + part[2] * shrink
            at = slice(block * top.shape[1], (block + 1) * top.shape[1])
            base_ref[head, 0:1, at] = top + jnp.log2(total) * (1.0 / EXP2_SCALE)
            delta_ref[head, 0:1, at] = dots / total


def grads_call(curs, hists, queries, stats, tiles, sums_in=None, last=False, whole=()):
    nk, nq = len(curs), len(queries)
    tokens, feat = queries[0].shape[1:]
    rows = tokens
    heads = feat // HS
    width = nq * tokens
    held = [a for pieces in tiles.values() for pair, _ in pieces for a in pair]

    def kernel(*refs):
        cur, refs = refs[:nk], refs[nk:]
        hist, refs = refs[:nk], refs[nk:]
        query, refs = refs[:nq], refs[nq:]
        stat, refs = refs[:4], refs[4:]
        held_refs, refs = list(refs[: len(held)]), refs[len(held) :]
        found = {
            block: [(held_refs.pop(0), held_refs.pop(0), blocks) for _, blocks in pieces]
            for block, pieces in tiles.items()
        }
        if sums_in is not None:
            old, refs = refs[0], refs[1:]
        key_out, sum_out = refs[:n_out], refs[n_out:-2]
        base, delta = refs[-2:]
        combine_stats(stat, base, delta, heads)

        def saved_tile(block, which, head):
            parts = {}
            for *pair, blocks in found[block]:
                for j, b in enumerate(blocks):
                    parts[b] = pair[which][head, :, j * tokens : (j + 1) * tokens]
            return jnp.concatenate([parts[b] for b in range(nq)], axis=1)

        def part(block, head, keys, values, asked, grads, lift, shift, bias):
            if block in found:
                scores, grad_scores = saved_tile(block, 0, head), saved_tile(block, 1, head)
            else:
                scores, grad_scores = rows_dot(keys, asked), rows_dot(values, grads)
                if bias is not None:
                    scores = scores + bias
            prob = jnp.exp2((scores - lift) * EXP2_SCALE)
            score_grad = (prob * (grad_scores - shift)).astype(BF16)
            grad_v = plain_dot(prob.astype(BF16), grads)
            grad_k = plain_dot(score_grad, asked) * SCALE
            return score_grad, (grad_k, grad_v)

        def step(head, _):
            lanes = head_lanes(head)
            asked, grads = wide(query, 0, lanes), wide(query, 1, lanes)
            lift, shift = base[head, 0:1, :], delta[head, 0:1, :]
            total = None if sums_in is None else old[head]
            for kb in range(nk):
                blocks = [
                    (cur[kb][0, :, lanes], cur[kb][1, :, lanes], None),
                    (
                        hist[kb][0:rows, lanes],
                        hist[kb][rows : 2 * rows, lanes],
                        dead_bias(hist[kb], rows, width),
                    ),
                ]
                all_scores = []
                for i, (keys, values, bias) in enumerate(blocks):
                    score_grad, both = part(
                        2 * kb + i, head, keys, values, asked, grads, lift, shift, bias
                    )
                    all_scores.append(score_grad)
                    for j in range(2):
                        at = firsts[kb]
                        if kb in whole:
                            key_out[at][2 * i + j, :, lanes] = both[j].astype(BF16)
                        else:
                            key_out[at + i][j, :, lanes] = both[j].astype(BF16)
                add = plain_dot(
                    jnp.concatenate([keys for keys, _, _ in blocks], axis=0).T,
                    jnp.concatenate(all_scores, axis=0),
                )
                total = add if total is None else total + add
            if last:
                for b in range(nq):
                    piece = total[:, b * tokens : (b + 1) * tokens] * SCALE
                    sum_out[b][:, lanes] = piece.T.astype(BF16)
            else:
                sum_out[0][head] = total
            return 0

        lax.fori_loop(0, heads, step, 0)

    blocks, firsts = [], []
    for kb in range(nk):
        firsts.append(len(blocks))
        if kb in whole:
            blocks.append(jax.ShapeDtypeStruct((4, rows, feat), BF16))
        else:
            blocks += [jax.ShapeDtypeStruct((2, rows, feat), BF16)] * 2
    n_out = len(blocks)
    if last:
        sums = [jax.ShapeDtypeStruct((tokens, feat), BF16)] * nq
    else:
        sums = [jax.ShapeDtypeStruct((heads, HS, width), F32)]
    args = list(curs) + list(hists) + list(queries) + list(stats) + held
    if sums_in is not None:
        args.append(sums_in)
    work = nk * 2 * rows * width
    outs = call(
        kernel,
        blocks + sums,
        args,
        flops=2 * 5 * 2 * work * feat,
        exps=work * heads,
        scratch=[pltpu.VMEM((heads, 8, width), F32)] * 2,
    )
    return list(outs[:n_out]), list(outs[n_out:])


def pack_call(arrays, key_hist, value_hist, hist_len, sizes):
    rows, columns = arrays[0].shape
    nx, nc = sizes[2:]
    old, feat = key_hist.shape
    n = len(arrays)

    def kernel(*refs):
        ins, (key_in, value_in, count), outs = refs[:n], refs[n : n + 3], refs[n + 3 :]
        same, other, hist, held, sem = outs
        copies = [pltpu.make_async_copy(ref, held.at[i], sem.at[i]) for i, ref in enumerate(ins)]
        copies.append(pltpu.make_async_copy(key_in, hist.at[pl.ds(0, old)], sem.at[n]))
        copies.append(pltpu.make_async_copy(value_in, hist.at[pl.ds(old, old)], sem.at[n + 1]))
        for copy in copies:
            copy.start()
        filled = jnp.full((16, feat), count[0], jnp.int32).astype(F32)
        hist[2 * old :, :] = filled.astype(BF16)
        x, core = lax.axis_index("x"), lax.axis_index("c")
        for i in range(n):
            copies[i].wait()
            for j, step in enumerate(X_STEPS):
                for k, out in enumerate((same, other)):
                    part = lax.rem(x + step, nx) * nc + lax.rem(core + k, nc)
                    at = pl.ds(pl.multiple_of(part * feat, feat), feat)
                    out[i // 2, j, i % 2] = held[i, :, at]
        copies[n].wait()
        copies[n + 1].wait()

    shape = jax.ShapeDtypeStruct((n // 2, nx, 2, rows, feat), BF16)
    return pl.pallas_call(
        kernel,
        out_shape=[shape, shape, jax.ShapeDtypeStruct((2 * old + 16, feat), BF16)],
        in_specs=[pl.BlockSpec(memory_space=pl.ANY)] * (n + 2)
        + [pl.BlockSpec(memory_space=pltpu.SMEM)],
        out_specs=[VMEM] * 3,
        scratch_shapes=[
            pltpu.VMEM((n, rows, columns), BF16),
            pltpu.SemaphoreType.DMA((n + 2,)),
        ],
        compiler_params=pltpu.CompilerParams(vmem_limit_bytes=PACK_LIMIT),
    )(*arrays, key_hist, value_hist, hist_len)


def merge_call(same, other):
    pairs, nx, two, rows, feat = same.shape

    def kernel(a, b, *outs):
        for i in range(pairs):
            for j in range(nx):
                outs[i * nx + j][:, 0:rows, :] = a[i, j]
                outs[i * nx + j][:, rows : 2 * rows, :] = b[i, j]

    shape = jax.ShapeDtypeStruct((two, 2 * rows, feat), BF16)
    outs = call(kernel, [shape] * (pairs * nx), [same, other])
    return [list(outs[i * nx : (i + 1) * nx]) for i in range(pairs)]


def stack_call(blocks):
    two, rows, feat = blocks[0].shape

    def kernel(*refs):
        for j, ref in enumerate(refs[:-1]):
            refs[-1][:, j * rows : (j + 1) * rows, :] = ref[...]

    shape = jax.ShapeDtypeStruct((two, len(blocks) * rows, feat), BF16)
    return call(kernel, shape, blocks)


def finish_call(pieces, other, sizes, parts, whole):
    nx, count, rows, feat = other.shape
    nc = sizes[3]
    old = whole[0].shape[1]
    n = len(parts)

    def kernel(*refs):
        mine, rest, refs = refs[:nx], refs[nx], refs[nx + 1 :]
        terms, outs, sums = refs[: -count - 2], refs[-count - 2 : -2], refs[-2:]
        x, core = lax.axis_index("x"), lax.axis_index("c")
        for i, out in enumerate(sums):
            total = sum(term[i].astype(F32) for term in terms[:n])
            total = total + sum(term[2 + i].astype(F32) for term in terms[n:])
            out[...] = total.astype(BF16)
        for j, step in enumerate(X_STEPS):
            for k in range(nc):
                part = lax.rem(x + step, nx) * nc + lax.rem(core + k, nc)
                at = pl.ds(pl.multiple_of(part * feat, feat), feat)
                for i, out in enumerate(outs):
                    out[:, at] = mine[j][i, 0:rows] if k == 0 else rest[j, i]

    shapes = [jax.ShapeDtypeStruct((rows, nx * nc * feat), BF16)] * count
    shapes += [jax.ShapeDtypeStruct((old, feat), BF16)] * 2
    return call(kernel, shapes, [*pieces, other, *parts, *whole])


def add_call(query_parts, cur_parts, pieces):
    tokens, feat = query_parts[0].shape
    rows = tokens // pieces
    nq = len(query_parts)

    def kernel(*refs):
        ins, outs = refs[:-pieces], refs[-pieces:]
        sums = [
            sum(ref[...].astype(F32) for ref in ins[:nq]),
            sum(ref[0].astype(F32) for ref in ins[nq:]),
            sum(ref[1].astype(F32) for ref in ins[nq:]),
        ]
        for i, total in enumerate(sums):
            low = total.astype(BF16)
            for j, out in enumerate(outs):
                out[i] = low[j * rows : (j + 1) * rows]

    shape = jax.ShapeDtypeStruct((3, rows, feat), BF16)
    return list(call(kernel, [shape] * pieces, list(query_parts) + list(cur_parts)))


def other_call(pieces):
    count, rows, feat = pieces[0].shape
    rows //= 2

    def kernel(*refs):
        for j, ref in enumerate(refs[:-1]):
            refs[-1][j] = ref[:, rows:, :]

    shape = jax.ShapeDtypeStruct((len(pieces), count, rows, feat), BF16)
    return call(kernel, shape, list(pieces))


def ring_moves(sizes):
    nz, ny, nx, nc = sizes

    def table(target):
        pairs = []
        for z in range(nz):
            for y in range(ny):
                for x in range(nx):
                    for c in range(nc):
                        tz, ty, tx, tc = target(z, y, x, c)
                        src = ((z * ny + y) * nx + x) * nc + c
                        dst = ((tz % nz) * ny + ty % ny) * nx + tx % nx
                        pairs.append((src, dst * nc + tc % nc))
        return pairs

    def keys(step):
        return table(lambda z, y, x, c: (z, y + step, x, c) if c == 0 else (z + step, y, x, c))

    def queries(step):
        return table(lambda z, y, x, c: (z + step, y, x, c) if c == 0 else (z, y + step, x, c))

    def chips(step):
        return table(lambda z, y, x, c: (z, y, x + step, c))

    def cores():
        return table(lambda z, y, x, c: (z, y, x, c + 1))

    return keys, queries, chips, cores


def make_shards(sizes):
    key_move, query_move, chip_move, core_move = ring_moves(sizes)

    def to_key(value, step):
        return lax.ppermute(value, AXES, key_move(step))

    def to_query(value, step):
        return lax.ppermute(value, AXES, query_move(step))

    def shards(query, key_cur, value_cur, d_out, key_hist, value_hist, hist_len):
        same, other, hist0 = pack_call(
            [query, d_out, key_cur, value_cur], key_hist, value_hist, hist_len, sizes
        )
        other = lax.ppermute(other, AXES, core_move())
        hists = [hist0] + [to_key(hist0, -o) for o in OFFSETS[1:]]
        asked, kept = merge_call(same, other)
        kept, hists[1], hists[2] = lax.optimization_barrier((kept, hists[1], hists[2]))

        def exchange(pieces):
            moved = [
                lax.ppermute(p, AXES, chip_move(d)) for p, d in zip(pieces[1:], X_STEPS[1:])
            ]
            return stack_call(pieces[:1] + moved)

        query0 = exchange(asked)
        queries = [query0] + [to_query(query0, -o) for o in OFFSETS[1:]]
        cur0 = exchange(kept)
        curs = [cur0] + [to_key(cur0, -o) for o in OFFSETS[1:]]
        every = (0, 1, 2, 3)
        ends, middle = (0, 3), (1, 2)
        state, kept_a = stats_call(
            curs[:1], hists, [queries[0], queries[3]], ends, saved=SAVED
        )
        state, kept_b = stats_call(curs[:1], hists, queries[1:3], middle, state, saved=SAVED)
        state, kept_c = stats_call(
            curs[1:], [], queries, every, state, fresh=False, saved=(0, 1, 2)
        )
        stats = [state] + [to_query(state, -o) for o in OFFSETS[1:]]
        held = {("cur", 1 + i): [(pair, every)] for i, pair in enumerate(kept_c)}
        for i, a, b in zip(SAVED, kept_a, kept_b):
            name = ("hist", i - 1) if i else ("cur", 0)
            held[name] = [(a, ends), (b, middle)]

        def tiles(*blocks):
            names = [(kind, b) for b in blocks for kind in ("cur", "hist")]
            return {i: held[name] for i, name in enumerate(names) if name in held}

        far, sums = grads_call(curs[3:], hists[3:], queries, stats, tiles(3), whole=(0,))
        far = to_key(far[0], 2)
        (near_cur, near_hist, near_p), sums = grads_call(
            curs[1:3], hists[1:3], queries, stats, tiles(1, 2), sums[0], whole=(1,)
        )
        near_cur, near_p = to_key(near_cur, OFFSETS[1]), to_key(near_p, OFFSETS[2])
        own, sums = grads_call(curs[:1], hists[:1], queries, stats, tiles(0), sums[0], True)
        sums, far = lax.optimization_barrier((sums, far))
        query_parts = [sums[0]] + [to_query(sums[i], OFFSETS[i]) for i in range(1, 4)]

        back = add_call(query_parts, [own[0], far, near_cur, near_p], sizes[2])
        back, near_hist = lax.optimization_barrier((back, near_hist))
        near_hist = to_key(near_hist, OFFSETS[1])
        moved = [lax.ppermute(p, AXES, chip_move(-d)) for p, d in zip(back[1:], X_STEPS[1:])]
        back = back[:1] + moved
        other = lax.ppermute(other_call(back), AXES, core_move())
        return tuple(finish_call(back, other, sizes, [own[1], near_hist], [far, near_p]))

    return shards


def solution(mesh):
    sizes = (4, 4, 4, 2)
    grid = Mesh(mesh.devices.reshape(sizes), AXES)
    token = P(AXES, None)
    hist = P(("z", "y"), ("x", "c"))
    return jax.shard_map(
        make_shards(sizes),
        mesh=grid,
        in_specs=(token, token, token, token, hist, hist, P(("z", "y"))),
        out_specs=(token, token, token, hist, hist),
        check_vma=False,
    )
```

```python
import math

import jax
import jax.numpy as jnp
from jax import lax
from jax.experimental import pallas as pl
from jax.experimental.pallas import tpu as pltpu
from jax.sharding import Mesh
from jax.sharding import PartitionSpec as P

HS = 128
SCALE = 1.0 / math.sqrt(HS)
EXP2_SCALE = SCALE * math.log2(math.e)
LOW = -1e30
VMEM_LIMIT = 6 * 1024 * 1024
PACK_LIMIT = 56 * 1024 * 1024
SAVED = (0, 1, 2, 4)
AXES = ("z", "y", "x", "c")
OFFSETS = (0, -1, 1, 2)
X_STEPS = (0, 1, 3, 2)
F32 = jnp.float32
BF16 = jnp.bfloat16
VMEM = pl.BlockSpec(memory_space=pltpu.VMEM)


def rows_dot(a, b):
    return lax.dot_general(a, b, (((1,), (1,)), ((), ())), preferred_element_type=F32)


def plain_dot(a, b):
    return lax.dot_general(a, b, (((1,), (0,)), ((), ())), preferred_element_type=F32)


def call(kernel, outs, args, flops=0, exps=0, scratch=()):
    size = sum(a.size * a.dtype.itemsize for a in args)
    return pl.pallas_call(
        kernel,
        out_shape=outs,
        in_specs=[VMEM] * len(args),
        out_specs=jax.tree.map(lambda _: VMEM, outs),
        scratch_shapes=list(scratch),
        compiler_params=pltpu.CompilerParams(vmem_limit_bytes=VMEM_LIMIT),
        cost_estimate=pl.CostEstimate(flops=flops // 64, bytes_accessed=size // 64, transcendentals=0),
    )(*args)


def head_lanes(head):
    return pl.ds(pl.multiple_of(head * HS, HS), HS)


def dead_bias(hist, rows, width):
    count = hist[2 * rows : 2 * rows + 16, 0:HS].astype(F32)[0:1]
    slot = lax.broadcasted_iota(jnp.int32, (rows, HS), 0).astype(F32)
    bias = jnp.where(slot < count, 0.0, LOW)
    return jnp.concatenate([bias] * (width // HS), axis=1)


def wide(blocks, which, lanes):
    return jnp.concatenate([block[which, :, lanes] for block in blocks], axis=0)


def stat_step(keys, values, queries, grads, state, bias, keep):
    top, total, dots = state
    scores = rows_dot(keys, queries)
    if bias is not None:
        scores = scores + bias
    new_top = jnp.maximum(top, jnp.max(scores, axis=0, keepdims=True))
    shrink = jnp.exp2((top - new_top) * EXP2_SCALE)
    weights = jnp.exp2((scores - new_top) * EXP2_SCALE)
    grad_scores = rows_dot(values, grads)
    total = total * shrink + jnp.sum(weights, axis=0, keepdims=True)
    dots = dots * shrink + jnp.sum(weights * grad_scores, axis=0, keepdims=True)
    if keep is not None:
        keep(scores, grad_scores)
    return new_top, total, dots


def stats_call(curs, hists, queries, at, state_in=None, fresh=True, saved=()):
    nk, nh, nq = len(curs), len(hists), len(queries)
    tokens, feat = queries[0].shape[1:]
    rows = tokens
    heads = feat // HS
    width = tokens * nq

    def kernel(*refs):
        cur, refs = refs[:nk], refs[nk:]
        hist, refs = refs[:nh], refs[nh:]
        query, refs = refs[:nq], refs[nq:]
        if state_in is not None:
            old, refs = refs[0], refs[1:]
        out, tiles = refs[0], refs[1:]
        if state_in is not None:
            out[...] = old[...]

        def step(head, _):
            lanes = head_lanes(head)
            asked, grads = wide(query, 0, lanes), wide(query, 1, lanes)
            places = [pl.ds(head * 4 + b, 1) for b in at]
            if fresh:
                low, zero = jnp.full((1, width), LOW, F32), jnp.zeros((1, width), F32)
                state = (low, zero, zero)
            else:
                state = tuple(
                    jnp.concatenate([old[i, row, :] for row in places], axis=1) for i in range(3)
                )

            def keep_of(block):
                if block not in saved:
                    return None
                i = saved.index(block)

                def keep(scores, grad_scores):
                    tiles[2 * i][head] = scores
                    tiles[2 * i + 1][head] = grad_scores

                return keep

            for i in range(nk):
                keys, values = cur[i][0, :, lanes], cur[i][1, :, lanes]
                state = stat_step(keys, values, asked, grads, state, None, keep_of(i))
            for i in range(nh):
                keys, values = hist[i][0:rows, lanes], hist[i][rows : 2 * rows, lanes]
                bias = dead_bias(hist[i], rows, width)
                state = stat_step(keys, values, asked, grads, state, bias, keep_of(nk + i))
            for i in range(3):
                for j, row in enumerate(places):
                    out[i, row, :] = state[i][:, j * tokens : (j + 1) * tokens]
            return 0

        lax.fori_loop(0, heads, step, 0)

    args = list(curs) + list(hists) + list(queries) + ([] if state_in is None else [state_in])
    work = (nk + nh) * rows * width
    outs = [jax.ShapeDtypeStruct((3, 16, tokens), F32)]
    outs += [jax.ShapeDtypeStruct((heads, rows, width), F32)] * (2 * len(saved))
    outs = call(kernel, outs, args, flops=2 * 2 * 2 * work * feat, exps=work * heads)
    return outs[0], [tuple(outs[1 + 2 * i : 3 + 2 * i]) for i in range(len(saved))]


def combine_stats(stats, base_ref, delta_ref, heads):
    for head in range(heads):
        for block, offset in enumerate(OFFSETS):
            parts = []
            for ref, step in zip(stats, OFFSETS):
                there = [o % 4 for o in OFFSETS].index((offset - step) % 4)
                row = head * 4 + there
                parts.append([ref[i, row : row + 1, :] for i in range(3)])
            top = jnp.maximum(
                jnp.maximum(parts[0][0], parts[1][0]), jnp.maximum(parts[2][0], parts[3][0])
            )
            total = jnp.zeros_like(top)
            dots = jnp.zeros_like(top)
            for part in parts:
                shrink = jnp.exp2((part[0] - top) * EXP2_SCALE)
                total = total + part[1] * shrink
                dots = dots + part[2] * shrink
            at = slice(block * top.shape[1], (block + 1) * top.shape[1])
            base_ref[head, 0:1, at] = top + jnp.log2(total) * (1.0 / EXP2_SCALE)
            delta_ref[head, 0:1, at] = dots / total


def grads_call(curs, hists, queries, stats, tiles, sums_in=None, last=False, whole=()):
    nk, nq = len(curs), len(queries)
    tokens, feat = queries[0].shape[1:]
    rows = tokens
    heads = feat // HS
    width = nq * tokens
    held = [a for pieces in tiles.values() for pair, _ in pieces for a in pair]

    def kernel(*refs):
        cur, refs = refs[:nk], refs[nk:]
        hist, refs = refs[:nk], refs[nk:]
        query, refs = refs[:nq], refs[nq:]
        stat, refs = refs[:4], refs[4:]
        held_refs, refs = list(refs[: len(held)]), refs[len(held) :]
        found = {
            block: [(held_refs.pop(0), held_refs.pop(0), blocks) for _, blocks in pieces]
            for block, pieces in tiles.items()
        }
        if sums_in is not None:
            old, refs = refs[0], refs[1:]
        key_out, sum_out = refs[:n_out], refs[n_out:-2]
        base, delta = refs[-2:]
        combine_stats(stat, base, delta, heads)

        def saved_tile(block, which, head):
            parts = {}
            for *pair, blocks in found[block]:
                for j, b in enumerate(blocks):
                    parts[b] = pair[which][head, :, j * tokens : (j + 1) * tokens]
            return jnp.concatenate([parts[b] for b in range(nq)], axis=1)

        def part(block, head, keys, values, asked, grads, lift, shift, bias):
            if block in found:
                scores, grad_scores = saved_tile(block, 0, head), saved_tile(block, 1, head)
            else:
                scores, grad_scores = rows_dot(keys, asked), rows_dot(values, grads)
                if bias is not None:
                    scores = scores + bias
            prob = jnp.exp2((scores - lift) * EXP2_SCALE)
            score_grad = (prob * (grad_scores - shift)).astype(BF16)
            grad_v = plain_dot(prob.astype(BF16), grads)
            grad_k = plain_dot(score_grad, asked) * SCALE
            return score_grad, (grad_k, grad_v)

        def step(head, _):
            lanes = head_lanes(head)
            asked, grads = wide(query, 0, lanes), wide(query, 1, lanes)
            lift, shift = base[head, 0:1, :], delta[head, 0:1, :]
            total = None if sums_in is None else old[head]
            for kb in range(nk):
                blocks = [
                    (cur[kb][0, :, lanes], cur[kb][1, :, lanes], None),
                    (
                        hist[kb][0:rows, lanes],
                        hist[kb][rows : 2 * rows, lanes],
                        dead_bias(hist[kb], rows, width),
                    ),
                ]
                all_scores = []
                for i, (keys, values, bias) in enumerate(blocks):
                    score_grad, both = part(
                        2 * kb + i, head, keys, values, asked, grads, lift, shift, bias
                    )
                    all_scores.append(score_grad)
                    for j in range(2):
                        at = firsts[kb]
                        if kb in whole:
                            key_out[at][2 * i + j, :, lanes] = both[j].astype(BF16)
                        else:
                            key_out[at + i][j, :, lanes] = both[j].astype(BF16)
                add = plain_dot(
                    jnp.concatenate([keys for keys, _, _ in blocks], axis=0).T,
                    jnp.concatenate(all_scores, axis=0),
                )
                total = add if total is None else total + add
            if last:
                for b in range(nq):
                    piece = total[:, b * tokens : (b + 1) * tokens] * SCALE
                    sum_out[b][:, lanes] = piece.T.astype(BF16)
            else:
                sum_out[0][head] = total
            return 0

        lax.fori_loop(0, heads, step, 0)

    blocks, firsts = [], []
    for kb in range(nk):
        firsts.append(len(blocks))
        if kb in whole:
            blocks.append(jax.ShapeDtypeStruct((4, rows, feat), BF16))
        else:
            blocks += [jax.ShapeDtypeStruct((2, rows, feat), BF16)] * 2
    n_out = len(blocks)
    if last:
        sums = [jax.ShapeDtypeStruct((tokens, feat), BF16)] * nq
    else:
        sums = [jax.ShapeDtypeStruct((heads, HS, width), F32)]
    args = list(curs) + list(hists) + list(queries) + list(stats) + held
    if sums_in is not None:
        args.append(sums_in)
    work = nk * 2 * rows * width
    outs = call(
        kernel,
        blocks + sums,
        args,
        flops=2 * 5 * 2 * work * feat,
        exps=work * heads,
        scratch=[pltpu.VMEM((heads, 8, width), F32)] * 2,
    )
    return list(outs[:n_out]), list(outs[n_out:])


def pack_call(arrays, key_hist, value_hist, hist_len, sizes):
    rows, columns = arrays[0].shape
    nx, nc = sizes[2:]
    old, feat = key_hist.shape
    n = len(arrays)

    def kernel(*refs):
        ins, (key_in, value_in, count), outs = refs[:n], refs[n : n + 3], refs[n + 3 :]
        same, other, hist, held, sem = outs
        copies = [pltpu.make_async_copy(ref, held.at[i], sem.at[i]) for i, ref in enumerate(ins)]
        copies.append(pltpu.make_async_copy(key_in, hist.at[pl.ds(0, old)], sem.at[n]))
        copies.append(pltpu.make_async_copy(value_in, hist.at[pl.ds(old, old)], sem.at[n + 1]))
        for copy in copies:
            copy.start()
        filled = jnp.full((16, feat), count[0], jnp.int32).astype(F32)
        hist[2 * old :, :] = filled.astype(BF16)
        x, core = lax.axis_index("x"), lax.axis_index("c")
        for i in range(n):
            copies[i].wait()
            for j, step in enumerate(X_STEPS):
                for k, out in enumerate((same, other)):
                    part = lax.rem(x + step, nx) * nc + lax.rem(core + k, nc)
                    at = pl.ds(pl.multiple_of(part * feat, feat), feat)
                    out[i // 2, j, i % 2] = held[i, :, at]
        copies[n].wait()
        copies[n + 1].wait()

    shape = jax.ShapeDtypeStruct((n // 2, nx, 2, rows, feat), BF16)
    return pl.pallas_call(
        kernel,
        out_shape=[shape, shape, jax.ShapeDtypeStruct((2 * old + 16, feat), BF16)],
        in_specs=[pl.BlockSpec(memory_space=pl.ANY)] * (n + 2)
        + [pl.BlockSpec(memory_space=pltpu.SMEM)],
        out_specs=[VMEM] * 3,
        scratch_shapes=[
            pltpu.VMEM((n, rows, columns), BF16),
            pltpu.SemaphoreType.DMA((n + 2,)),
        ],
        compiler_params=pltpu.CompilerParams(vmem_limit_bytes=PACK_LIMIT),
    )(*arrays, key_hist, value_hist, hist_len)


def merge_call(same, other):
    pairs, nx, two, rows, feat = same.shape

    def kernel(a, b, *outs):
        for i in range(pairs):
            for j in range(nx):
                outs[i * nx + j][:, 0:rows, :] = a[i, j]
                outs[i * nx + j][:, rows : 2 * rows, :] = b[i, j]

    shape = jax.ShapeDtypeStruct((two, 2 * rows, feat), BF16)
    outs = call(kernel, [shape] * (pairs * nx), [same, other])
    return [list(outs[i * nx : (i + 1) * nx]) for i in range(pairs)]


def stack_call(blocks):
    two, rows, feat = blocks[0].shape

    def kernel(*refs):
        for j, ref in enumerate(refs[:-1]):
            refs[-1][:, j * rows : (j + 1) * rows, :] = ref[...]

    shape = jax.ShapeDtypeStruct((two, len(blocks) * rows, feat), BF16)
    return call(kernel, shape, blocks)


def finish_call(pieces, other, sizes, parts, whole):
    nx, count, rows, feat = other.shape
    nc = sizes[3]
    old = whole[0].shape[1]
    n = len(parts)

    def kernel(*refs):
        mine, rest, refs = refs[:nx], refs[nx], refs[nx + 1 :]
        terms, outs, sums = refs[: -count - 2], refs[-count - 2 : -2], refs[-2:]
        x, core = lax.axis_index("x"), lax.axis_index("c")
        for i, out in enumerate(sums):
            total = sum(term[i].astype(F32) for term in terms[:n])
            total = total + sum(term[2 + i].astype(F32) for term in terms[n:])
            out[...] = total.astype(BF16)
        for j, step in enumerate(X_STEPS):
            for k in range(nc):
                part = lax.rem(x + step, nx) * nc + lax.rem(core + k, nc)
                at = pl.ds(pl.multiple_of(part * feat, feat), feat)
                for i, out in enumerate(outs):
                    out[:, at] = mine[j][i, 0:rows] if k == 0 else rest[j, i]

    shapes = [jax.ShapeDtypeStruct((rows, nx * nc * feat), BF16)] * count
    shapes += [jax.ShapeDtypeStruct((old, feat), BF16)] * 2
    return call(kernel, shapes, [*pieces, other, *parts, *whole])


def add_call(query_parts, cur_parts, pieces):
    tokens, feat = query_parts[0].shape
    rows = tokens // pieces
    nq = len(query_parts)

    def kernel(*refs):
        ins, outs = refs[:-pieces], refs[-pieces:]
        sums = [
            sum(ref[...].astype(F32) for ref in ins[:nq]),
            sum(ref[0].astype(F32) for ref in ins[nq:]),
            sum(ref[1].astype(F32) for ref in ins[nq:]),
        ]
        for i, total in enumerate(sums):
            low = total.astype(BF16)
            for j, out in enumerate(outs):
                out[i] = low[j * rows : (j + 1) * rows]

    shape = jax.ShapeDtypeStruct((3, rows, feat), BF16)
    return list(call(kernel, [shape] * pieces, list(query_parts) + list(cur_parts)))


def other_call(pieces):
    count, rows, feat = pieces[0].shape
    rows //= 2

    def kernel(*refs):
        for j, ref in enumerate(refs[:-1]):
            refs[-1][j] = ref[:, rows:, :]

    shape = jax.ShapeDtypeStruct((len(pieces), count, rows, feat), BF16)
    return call(kernel, shape, list(pieces))


def ring_moves(sizes):
    nz, ny, nx, nc = sizes

    def table(target):
        pairs = []
        for z in range(nz):
            for y in range(ny):
                for x in range(nx):
                    for c in range(nc):
                        tz, ty, tx, tc = target(z, y, x, c)
                        src = ((z * ny + y) * nx + x) * nc + c
                        dst = ((tz % nz) * ny + ty % ny) * nx + tx % nx
                        pairs.append((src, dst * nc + tc % nc))
        return pairs

    def keys(step):
        return table(lambda z, y, x, c: (z, y + step, x, c) if c == 0 else (z + step, y, x, c))

    def queries(step):
        return table(lambda z, y, x, c: (z + step, y, x, c) if c == 0 else (z, y + step, x, c))

    def chips(step):
        return table(lambda z, y, x, c: (z, y, x + step, c))

    def cores():
        return table(lambda z, y, x, c: (z, y, x, c + 1))

    return keys, queries, chips, cores


def make_shards(sizes):
    key_move, query_move, chip_move, core_move = ring_moves(sizes)

    def to_key(value, step):
        return lax.ppermute(value, AXES, key_move(step))

    def to_query(value, step):
        return lax.ppermute(value, AXES, query_move(step))

    def shards(query, key_cur, value_cur, d_out, key_hist, value_hist, hist_len):
        same, other, hist0 = pack_call(
            [query, d_out, key_cur, value_cur], key_hist, value_hist, hist_len, sizes
        )
        other = lax.ppermute(other, AXES, core_move())
        hists = [hist0] + [to_key(hist0, -o) for o in OFFSETS[1:]]
        asked, kept = merge_call(same, other)
        kept, hists[1], hists[2] = lax.optimization_barrier((kept, hists[1], hists[2]))

        def exchange(pieces):
            moved = [
                lax.ppermute(p, AXES, chip_move(d)) for p, d in zip(pieces[1:], X_STEPS[1:])
            ]
            return stack_call(pieces[:1] + moved)

        query0 = exchange(asked)
        queries = [query0] + [to_query(query0, -o) for o in OFFSETS[1:]]
        cur0 = exchange(kept)
        curs = [cur0] + [to_key(cur0, -o) for o in OFFSETS[1:]]
        every = (0, 1, 2, 3)
        ends, middle = (0, 3), (1, 2)
        state, kept_a = stats_call(
            curs[:1], hists, [queries[0], queries[3]], ends, saved=SAVED
        )
        state, kept_b = stats_call(curs[:1], hists, queries[1:3], middle, state, saved=SAVED)
        state, kept_c = stats_call(
            curs[1:], [], queries, every, state, fresh=False, saved=(0, 1, 2)
        )
        stats = [state] + [to_query(state, -o) for o in OFFSETS[1:]]
        held = {("cur", 1 + i): [(pair, every)] for i, pair in enumerate(kept_c)}
        for i, a, b in zip(SAVED, kept_a, kept_b):
            name = ("hist", i - 1) if i else ("cur", 0)
            held[name] = [(a, ends), (b, middle)]

        def tiles(*blocks):
            names = [(kind, b) for b in blocks for kind in ("cur", "hist")]
            return {i: held[name] for i, name in enumerate(names) if name in held}

        far, sums = grads_call(curs[3:], hists[3:], queries, stats, tiles(3), whole=(0,))
        far = to_key(far[0], 2)
        (near_cur, near_hist, near_p), sums = grads_call(
            curs[1:3], hists[1:3], queries, stats, tiles(1, 2), sums[0], whole=(1,)
        )
        near_cur, near_p = to_key(near_cur, OFFSETS[1]), to_key(near_p, OFFSETS[2])
        own, sums = grads_call(curs[:1], hists[:1], queries, stats, tiles(0), sums[0], True)
        query_parts = [sums[0]] + [to_query(sums[i], OFFSETS[i]) for i in range(1, 4)]

        back = add_call(query_parts, [own[0], far, near_cur, near_p], sizes[2])
        back, near_hist = lax.optimization_barrier((back, near_hist))
        near_hist = to_key(near_hist, OFFSETS[1])
        moved = [lax.ppermute(p, AXES, chip_move(-d)) for p, d in zip(back[1:], X_STEPS[1:])]
        back = back[:1] + moved
        other = lax.ppermute(other_call(back), AXES, core_move())
        return tuple(finish_call(back, other, sizes, [own[1], near_hist], [far, near_p]))

    return shards


def solution(mesh):
    sizes = (4, 4, 4, 2)
    grid = Mesh(mesh.devices.reshape(sizes), AXES)
    token = P(AXES, None)
    hist = P(("z", "y"), ("x", "c"))
    return jax.shard_map(
        make_shards(sizes),
        mesh=grid,
        in_specs=(token, token, token, token, hist, hist, P(("z", "y"))),
        out_specs=(token, token, token, hist, hist),
        check_vma=False,
    )
```
